128 devices in a mesh: chan: 32 (over z, y, x_hi), tm: 4 (over x_lo, core).
Axes of the slice: x: 4 (x_hi: 2, x_lo: 2; x = x_hi * 2 + x_lo), y: 4, z: 4, core: 2. Of those that a mesh axis runs over, the one named last changes fastest.
Arguments:
- visibilities: bfloat16 [64, 16, 2, 512, 512], P('chan', 'tm'), may hold values from -640 to 640, as said below
- model: bfloat16 [64, 16, 2, 512, 512], P('chan', 'tm'), may hold values from -32 to 32, as said below
- beam_left: bfloat16 [8, 256, 128], replicated, may hold values from -0.5 to 0.5
- beam_right: bfloat16 [8, 256, 128], replicated, may hold values from -0.01171875 to 0.01171875
- weight_index: int32 [64, 16], P('chan'), may hold values from 0 to 7
- target_bank: int32 [64, 16, 16], P('chan', 'tm'), may hold values from 0 to 7
- widths: int32 [64], P('chan'), may hold values from 0 to 2, as said below
Outputs:
- covariance: float32 [4096, 256], P('chan')
The draws below stay inside these ranges and needn't reach their ends.
Inputs may be any that keep to these rules, and one draw needn't show every extreme that they name: `visibilities`: real part at index 0 and imaginary part at index 1; each matrix is Hermitian in its last two dimensions. `model`: real part at index 0 and imaginary part at index 1; each matrix is Hermitian in its last two dimensions. `widths`: some channel has width 2.
All inputs are finite; a program needn't handle non-finite values.
Results may differ from the reference program's by a relative error of at most 0.0041.
Values sent between devices are 32-bit elements; how exact they have to be, the bound alone decides.
A program may use at most 256 MiB of HBM per device.

```python
import math
import jax
import jax.numpy as jnp
from jax import lax

N = 512
BLK = 128
BEAMS = 256
BANKS = 8
NWEIGHT = 8
ITERS = 6
HW = 2
CHANNELS = 64
INTERVALS = 16
NBLK = 16


def joint_draw(key):
    keys = jax.random.split(key, 9)
    shape = (CHANNELS, INTERVALS, N, N)
    raw_re = jax.random.truncated_normal(keys[0], -4.0, 4.0, shape, jnp.float32)
    raw_im = jax.random.truncated_normal(keys[1], -4.0, 4.0, shape, jnp.float32)
    mod_re = 0.5 * (raw_re + jnp.swapaxes(raw_re, -1, -2))
    mod_im = 0.5 * (raw_im - jnp.swapaxes(raw_im, -1, -2))
    base_amp = jnp.exp(jax.random.uniform(keys[3], (CHANNELS, 1, N), jnp.float32, math.log(0.5), math.log(2.0)))
    amplitude = base_amp * jnp.exp(0.15 * jax.random.truncated_normal(keys[4], -4.0, 4.0, (CHANNELS, INTERVALS, N), jnp.float32))
    phase = jax.random.uniform(keys[5], (CHANNELS, 1, N), jnp.float32, -math.pi, math.pi)
    phase = phase + 0.3 * jax.random.truncated_normal(keys[6], -4.0, 4.0, (CHANNELS, INTERVALS, N), jnp.float32)
    gain_re = amplitude * jnp.cos(phase)
    gain_im = amplitude * jnp.sin(phase)
    noise_re = 0.1 * jax.random.truncated_normal(keys[7], -4.0, 4.0, shape, jnp.float32)
    noise_im = 0.1 * jax.random.truncated_normal(keys[8], -4.0, 4.0, shape, jnp.float32)
    noise_re = noise_re + jnp.swapaxes(noise_re, -1, -2)
    noise_im = noise_im - jnp.swapaxes(noise_im, -1, -2)
    left_re = gain_re[..., :, None] * mod_re - gain_im[..., :, None] * mod_im
    left_im = gain_re[..., :, None] * mod_im + gain_im[..., :, None] * mod_re
    vis_re = left_re * gain_re[..., None, :] + left_im * gain_im[..., None, :] + noise_re
    vis_im = left_im * gain_re[..., None, :] - left_re * gain_im[..., None, :] + noise_im
    model_pair = jnp.stack([mod_re, mod_im], axis=2)
    vis_pair = jnp.stack([vis_re, vis_im], axis=2)
    return (model_pair, vis_pair)


def draw_visibilities(key, part):
    model_pair, vis_pair = joint_draw(key)
    return vis_pair.astype(jnp.bfloat16)


def draw_model(key, part):
    model_pair, vis_pair = joint_draw(key)
    return model_pair.astype(jnp.bfloat16)


def draw_widths(key, part):
    key = jax.random.fold_in(key, 7)
    first_key, second_key = jax.random.split(key, 2)
    drawn = jax.random.randint(first_key, (CHANNELS,), 0, HW + 1, jnp.int32)
    chosen = jax.random.randint(second_key, (), 0, CHANNELS, jnp.int32)
    return jnp.where(jnp.arange(CHANNELS, dtype=jnp.int32) == chosen, HW, drawn).astype(jnp.int32)


def place_ends(values, stream_key, low, top_value):
    dims = values.shape
    spot = [jax.random.randint(jax.random.fold_in(stream_key, axis), (), 0, dims[axis]) for axis in range(len(dims))]
    values = values.at[tuple(spot)].set(low)
    longest = dims.index(max(dims))
    spot[longest] = (spot[longest] + 1) % dims[longest]
    return values.at[tuple(spot)].set(top_value)


def centred(rng, dims, scale, most, kind=jnp.bfloat16):
    entries = jax.random.normal(rng, dims, jnp.float32) * scale
    return jnp.minimum(jnp.maximum(entries, -most), most).astype(kind)


def setup_inputs(seed: int = 0) -> dict:
    streams_of = jax.random.split(jax.random.key(seed), 8)
    return {
        "visibilities": draw_visibilities(jax.random.fold_in(streams_of[7], 71), 0),
        "model": draw_model(jax.random.fold_in(streams_of[7], 71), 0),
        "beam_left": centred(streams_of[2], (NWEIGHT, BEAMS, BLK), BLK ** -0.5, 0.5),
        "beam_right": centred(streams_of[3], (NWEIGHT, BEAMS, BLK), (BLK * CHANNELS * INTERVALS * NBLK // BANKS) ** -0.5, 0.01171875),
        "weight_index": place_ends(jax.random.randint(streams_of[4], (CHANNELS, NBLK), 0, NWEIGHT), jax.random.fold_in(streams_of[4], 1), 0, NWEIGHT - 1).astype(jnp.int32),
        "target_bank": place_ends(jax.random.randint(streams_of[5], (CHANNELS, INTERVALS, NBLK), 0, BANKS), jax.random.fold_in(streams_of[5], 1), 0, BANKS - 1).astype(jnp.int32),
        "widths": draw_widths(jax.random.fold_in(streams_of[7], 71), 0),
    }


epsilon = 1e-06

def contract(vector, matrix):
    return jnp.einsum('...q,...qp->...p', vector, matrix, precision=lax.Precision.HIGHEST)

def stefcal(visibilities, model):
    vis_re = visibilities[..., 0, :, :].astype(jnp.float32)
    vis_im = visibilities[..., 1, :, :].astype(jnp.float32)
    mod_re = model[..., 0, :, :].astype(jnp.float32)
    mod_im = model[..., 1, :, :].astype(jnp.float32)
    cross_re = mod_re * vis_re + mod_im * vis_im
    cross_im = mod_im * vis_re - mod_re * vis_im
    power = mod_re * mod_re + mod_im * mod_im
    gain_re = jnp.ones(vis_re.shape[:-1], jnp.float32)
    gain_im = jnp.zeros(vis_re.shape[:-1], jnp.float32)
    for sweep_index in range(ITERS):
        num_re = contract(gain_re, cross_re) - contract(gain_im, cross_im)
        num_im = contract(gain_re, cross_im) + contract(gain_im, cross_re)
        denominator = contract(gain_re * gain_re + gain_im * gain_im, power) + epsilon
        new_re = num_re / denominator
        new_im = num_im / denominator
        if sweep_index % 2 == 1:
            gain_re = 0.5 * (new_re + gain_re)
            gain_im = 0.5 * (new_im + gain_im)
        else:
            gain_re = new_re
            gain_im = new_im
    return (gain_re, gain_im)

def align_phase(gain_re, gain_im):
    first_re = gain_re[..., :1]
    first_im = gain_im[..., :1]
    divisor = jnp.maximum(jnp.sqrt(first_re * first_re + first_im * first_im), 1.0)
    unit_re = first_re / divisor
    unit_im = -first_im / divisor
    return (gain_re * unit_re - gain_im * unit_im, gain_re * unit_im + gain_im * unit_re)

def calibrate(smooth_re, smooth_im, visibilities):
    vis_re = visibilities[..., 0, :, :].astype(jnp.float32)
    vis_im = visibilities[..., 1, :, :].astype(jnp.float32)
    denominator = jnp.maximum(smooth_re * smooth_re + smooth_im * smooth_im, 1.0)
    inv_re = smooth_re / denominator
    inv_im = -smooth_im / denominator
    row_re = inv_re[..., :, None]
    row_im = inv_im[..., :, None]
    col_re = inv_re[..., None, :]
    col_im = inv_im[..., None, :]
    left_re = row_re * vis_re - row_im * vis_im
    left_im = row_re * vis_im + row_im * vis_re
    out_re = left_re * col_re + left_im * col_im
    out_im = left_im * col_re - left_re * col_im
    return jnp.stack([out_re, out_im], axis=-3).astype(jnp.bfloat16)

def smooth_time(ref_re, ref_im, width):
    interval = jnp.arange(INTERVALS)
    padded_re = jnp.pad(ref_re, ((HW, HW), (0, 0)))
    padded_im = jnp.pad(ref_im, ((HW, HW), (0, 0)))
    summed_re = jnp.zeros_like(ref_re)
    summed_im = jnp.zeros_like(ref_im)
    counts = jnp.zeros((INTERVALS,), jnp.float32)
    for offset in range(-HW, HW + 1):
        inside = ((abs(offset) <= width) & (interval + offset >= 0) & (interval + offset < INTERVALS)).astype(jnp.float32)
        summed_re = summed_re + inside[:, None] * padded_re[HW + offset:HW + offset + INTERVALS]
        summed_im = summed_im + inside[:, None] * padded_im[HW + offset:HW + offset + INTERVALS]
        counts = counts + inside
    return (summed_re / counts[:, None], summed_im / counts[:, None])

def beam_channel(calibrated, left, right):
    group_count = N // BLK
    pieces = calibrated.astype(jnp.float32).reshape((-1, 2, group_count, BLK, group_count, BLK))
    left_groups = left.astype(jnp.float32).reshape((group_count, group_count, BEAMS, BLK))
    right_groups = right.astype(jnp.float32).reshape((group_count, group_count, BEAMS, BLK))
    formed = jnp.einsum('ijux,tsixjy->tijsuy', left_groups, pieces).astype(jnp.bfloat16)
    contrib = jnp.einsum('tijsuy,ijvy->tijsuv', formed.astype(jnp.float32), right_groups)
    return contrib.reshape((-1, 2, BEAMS, BEAMS))

def reference(visibilities, model, beam_left, beam_right, weight_index, target_bank, widths):

    def per_channel(accumulated, channel_data):
        vis_one, model_one, weight_one, banks_one, width_one = channel_data
        gain_re, gain_im = stefcal(vis_one, model_one)
        ref_re, ref_im = align_phase(gain_re, gain_im)
        smooth_re, smooth_im = smooth_time(ref_re, ref_im, width_one)
        calibrated = calibrate(smooth_re, smooth_im, vis_one)
        contrib = beam_channel(calibrated, beam_left[weight_one], beam_right[weight_one])
        accumulated = accumulated.at[banks_one.reshape(-1)].add(contrib)
        return (accumulated, None)
    start_banks = jnp.zeros((BANKS, 2, BEAMS, BEAMS), jnp.float32)
    final_banks, unused = lax.scan(per_channel, start_banks, (visibilities, model, weight_index, target_bank, widths))
    return final_banks.reshape((BANKS * 2 * BEAMS, BEAMS))
```

```python
import jax
import jax.numpy as jnp
from jax import lax
from jax.experimental import pallas as pl
from jax.experimental.pallas import tpu as pltpu
from jax.sharding import PartitionSpec as P

N = 512
BLK = 128
BEAMS = 256
BANKS = 8
NWEIGHT = 8
ITERS = 6
HW = 2
LC = 2
LT = 4
TMS = 4
ALL_T = 16
MATS = LC * LT
MESH = pl.DeviceIdType.MESH
MIB = 1024 * 1024
F32 = jnp.float32
BF16 = jnp.bfloat16

epsilon = 1e-06


def split(x):
    high = x.astype(BF16).astype(F32)
    return high, x - high


def gains_kernel(vis_ref, mod_ref, out_ref, mats):
    step = pl.program_id(0)
    strip = 64
    for top in range(0, N, strip):
        rows = slice(top, top + strip)
        vis_re = vis_ref[0, 0, rows, :].astype(F32)
        vis_im = vis_ref[0, 1, rows, :].astype(F32)
        mod_re = mod_ref[0, 0, rows, :].astype(F32)
        mod_im = mod_ref[0, 1, rows, :].astype(F32)
        mats[step, 0, rows, :] = (mod_re * vis_re + mod_im * vis_im).astype(BF16)
        mats[step, 1, rows, :] = (mod_im * vis_re - mod_re * vis_im).astype(BF16)
        mats[step, 2, rows, :] = (mod_re * mod_re + mod_im * mod_im).astype(BF16)

    @pl.when(step == MATS - 1)
    def _():
        row = lax.broadcasted_iota(jnp.int32, (MATS, N), 0)

        def sweep(k, gains):
            gain_re, gain_im = gains
            power = gain_re * gain_re + gain_im * gain_im
            both = jnp.concatenate([*split(gain_re), *split(gain_im)], axis=0).astype(BF16)
            size = jnp.concatenate(split(power), axis=0).astype(BF16)
            num_re = jnp.zeros((MATS, N), F32)
            num_im = jnp.zeros((MATS, N), F32)
            den = jnp.zeros((MATS, N), F32)
            for m in range(MATS):
                with_re = jnp.dot(both, mats[m, 0], preferred_element_type=F32)
                with_im = jnp.dot(both, mats[m, 1], preferred_element_type=F32)
                with_pw = jnp.dot(size, mats[m, 2], preferred_element_type=F32)
                one_re = (with_re[0:8] + with_re[8:16]) - (with_im[16:24] + with_im[24:32])
                one_im = (with_im[0:8] + with_im[8:16]) + (with_re[16:24] + with_re[24:32])
                mine = row == m
                num_re = jnp.where(mine, one_re, num_re)
                num_im = jnp.where(mine, one_im, num_im)
                den = jnp.where(mine, with_pw[0:8] + with_pw[8:16], den)
            den = den + epsilon
            new_re = num_re / den
            new_im = num_im / den
            odd = lax.rem(k, 2) == 1
            gain_re = jnp.where(odd, 0.5 * (new_re + gain_re), new_re)
            gain_im = jnp.where(odd, 0.5 * (new_im + gain_im), new_im)
            return gain_re, gain_im

        start = (jnp.ones((MATS, N), F32), jnp.zeros((MATS, N), F32))
        gain_re, gain_im = lax.fori_loop(0, ITERS, sweep, start)
        first_re = gain_re[:, 0:1]
        first_im = gain_im[:, 0:1]
        divisor = jnp.maximum(jnp.sqrt(first_re * first_re + first_im * first_im), 1.0)
        unit_re = first_re / divisor
        unit_im = -first_im / divisor
        out_ref[0] = gain_re * unit_re - gain_im * unit_im
        out_ref[1] = gain_re * unit_im + gain_im * unit_re


def referenced_gains(vis, mod):
    block = pl.BlockSpec((1, 2, N, N), lambda m: (m, 0, 0, 0))
    return pl.pallas_call(
        gains_kernel,
        grid=(MATS,),
        in_specs=[block, block],
        out_specs=pl.BlockSpec((2, MATS, N), lambda m: (0, 0, 0)),
        out_shape=jax.ShapeDtypeStruct((2, MATS, N), F32),
        scratch_shapes=[pltpu.VMEM((MATS, 3, N, N), BF16)],
        compiler_params=pltpu.CompilerParams(vmem_limit_bytes=40 * MIB),
        name="gains",
    )(vis, mod)


def smooth_kernel(width_ref, ref_ref, out_ref, halo, send_sem, recv_sem):
    me = lax.axis_index("tm")
    chan = lax.axis_index("chan")
    right = (chan, lax.rem(me + 1, TMS))
    left = (chan, lax.rem(me + TMS - 1, TMS))
    barrier = pltpu.get_barrier_semaphore()
    for other in (left, right):
        pl.semaphore_signal(barrier, inc=1, device_id=other, device_id_type=MESH)
    pl.semaphore_wait(barrier, 2)
    copies = [
        pltpu.make_async_remote_copy(
            src_ref=ref_ref,
            dst_ref=halo.at[slot],
            send_sem=send_sem.at[slot],
            recv_sem=recv_sem.at[slot],
            device_id=other,
            device_id_type=MESH,
        )
        for slot, other in ((0, right), (1, left))
    ]
    for copy in copies:
        copy.start()
    row = lax.broadcasted_iota(jnp.int32, (MATS, N), 0)
    within = lax.rem(row, LT)
    interval = me * LT + within
    width = jnp.where(row < LT, width_ref[0], width_ref[1])
    for copy in copies:
        copy.wait()

    def moved(x, offset):
        return x if offset % MATS == 0 else jnp.concatenate([x[offset % MATS :], x[: offset % MATS]], axis=0)

    sums = []
    for part in range(2):
        here = ref_ref[part]
        before = halo[0, part]
        after = halo[1, part]
        total = jnp.zeros((MATS, N), F32)
        count = jnp.zeros((MATS, N), F32)
        for offset in range(-HW, HW + 1):
            value = moved(here, offset)
            if offset > 0:
                value = jnp.where(within + offset < LT, value, moved(after, offset - LT))
            if offset < 0:
                value = jnp.where(within + offset >= 0, value, moved(before, offset + LT))
            inside = (width >= abs(offset)) & (interval + offset >= 0) & (interval + offset < ALL_T)
            total = total + jnp.where(inside, value, 0.0)
            count = count + jnp.where(inside, 1.0, 0.0)
        sums.append(total / count)
    smooth_re, smooth_im = sums
    size = jnp.maximum(smooth_re * smooth_re + smooth_im * smooth_im, 1.0)
    out_ref[0] = smooth_re / size
    out_ref[1] = -smooth_im / size


def inverse_gains(referenced, widths):
    return pl.pallas_call(
        smooth_kernel,
        in_specs=[
            pl.BlockSpec(memory_space=pltpu.SMEM),
            pl.BlockSpec(memory_space=pltpu.VMEM),
        ],
        out_specs=pl.BlockSpec(memory_space=pltpu.VMEM),
        out_shape=jax.ShapeDtypeStruct((2, MATS, N), F32),
        scratch_shapes=[
            pltpu.VMEM((2, 2, MATS, N), F32),
            pltpu.SemaphoreType.DMA((2,)),
            pltpu.SemaphoreType.DMA((2,)),
        ],
        compiler_params=pltpu.CompilerParams(collective_id=0, has_side_effects=True),
        name="smooth",
    )(widths, referenced)


def sums_kernel(weight_ref, bank_ref, inv_ref, vis_ref, out_ref):
    step = pl.program_id(0)

    @pl.when(step == 0)
    def _():
        def clear(k, carry):
            out_ref[k] = jnp.zeros((BLK, 2 * BLK), F32)
            return carry

        lax.fori_loop(0, BANKS * NWEIGHT, clear, 0)

    re = inv_ref[0, pl.ds(step, 1), :]
    im = inv_ref[1, pl.ds(step, 1), :]
    re_high, re_low = split(re)
    im_high, im_low = split(im)
    row = lax.broadcasted_iota(jnp.int32, (16, N), 0)

    def stacked(rows):
        out = jnp.zeros((16, N), F32)
        for k, one in enumerate(rows):
            out = jnp.where(row == k, one, out)
        return out

    by_row_re = stacked([re_high, re_low, re_high, im_high, im_low, im_high]).astype(BF16)
    by_row_im = stacked([im_high, im_low, im_high, -re_high, -re_low, -re_high]).astype(BF16)
    by_col = stacked([re_high, re_high, re_low, im_high, im_high, im_low]).astype(BF16)
    depth_first = (((0,), (0,)), ((), ()))
    groups = N // BLK
    for i in range(groups):
        rows = slice(i * BLK, (i + 1) * BLK)
        scale_re = lax.dot_general(by_row_re[:, rows], by_col, depth_first, preferred_element_type=F32)
        scale_im = lax.dot_general(by_row_im[:, rows], by_col, depth_first, preferred_element_type=F32)
        for j in range(groups):
            cols = slice(j * BLK, (j + 1) * BLK)
            place = bank_ref[step, i * groups + j] * NWEIGHT + weight_ref[step // LT, i * groups + j]
            vis_re = vis_ref[0, 0, rows, cols].astype(F32)
            vis_im = vis_ref[0, 1, rows, cols].astype(F32)
            one_re = scale_re[:, cols]
            one_im = scale_im[:, cols]
            out_ref[place, :, 0:BLK] += one_re * vis_re - one_im * vis_im
            out_ref[place, :, BLK : 2 * BLK] += one_re * vis_im + one_im * vis_re


def calibrated_sums(weight_index, target_bank, inverse, vis):
    return pl.pallas_call(
        sums_kernel,
        grid=(MATS,),
        in_specs=[
            pl.BlockSpec(memory_space=pltpu.SMEM),
            pl.BlockSpec(memory_space=pltpu.SMEM),
            pl.BlockSpec((2, MATS, N), lambda m: (0, 0, 0)),
            pl.BlockSpec((1, 2, N, N), lambda m: (m, 0, 0, 0)),
        ],
        out_specs=pl.BlockSpec((BANKS * NWEIGHT, BLK, 2 * BLK), lambda m: (0, 0, 0)),
        out_shape=jax.ShapeDtypeStruct((BANKS * NWEIGHT, BLK, 2 * BLK), F32),
        compiler_params=pltpu.CompilerParams(vmem_limit_bytes=40 * MIB),
        name="sums",
    )(weight_index, target_bank, inverse, vis)


ORDERS = (("x", "y", "z"), ("y", "z", "x"), ("z", "x", "y"))
TILES = ((0, 3), (3, 6), (6, 8))
COUNTS = tuple(high - low for low, high in TILES)


def beams_kernel(left_ref, right_ref, sums_ref, out_ref, *scratch):
    (held, lefts, rights, formed, terms, pair) = scratch[0:6]
    parts = scratch[6:9]
    relays = scratch[9:12]
    firsts = scratch[12:15]
    owns1 = scratch[15:18]
    seconds = scratch[18:21]
    owns2 = scratch[21:24]
    thirds = scratch[24:27]
    share = scratch[27]
    (load_sem, s0, r0, s1, r1, s2, r2, s3, r3, s4, r4) = scratch[28:39]

    chan = lax.axis_index("chan")
    tm = lax.axis_index("tm")
    z = lax.div(chan, 8)
    y = lax.rem(lax.div(chan, 2), 4)
    x_low = lax.div(tm, 2)
    x = lax.rem(chan, 2) * 2 + x_low
    core = lax.rem(tm, 2)
    place = {"x": x, "y": y, "z": z}

    def device(at, which=core):
        return (
            (at["z"] * 4 + at["y"]) * 2 + lax.div(at["x"], 2),
            lax.rem(at["x"], 2) * 2 + which,
        )

    def along(axis, by):
        return device({**place, axis: lax.rem(place[axis] + by, 4)})

    twin = device(place, 1 - core)
    other_low = lax.div(x, 2) * 2 + (1 - x_low)
    side = device({**place, "x": other_low})
    cross = device({**place, "x": other_low}, 1 - core)

    barrier = pltpu.get_barrier_semaphore()
    partners = [twin, cross] + [along(axis, by) for axis in "xyz" for by in (1, 2, 3)]
    for other in partners:
        pl.semaphore_signal(barrier, inc=1, device_id=other, device_id_type=MESH)

    def load(k):
        rows = pl.ds(k * NWEIGHT, NWEIGHT)
        return pltpu.make_async_copy(sums_ref.at[rows], held.at[rows], load_sem.at[k])

    for k in range(BANKS):
        load(k).start()
    for w in range(NWEIGHT):
        lefts[w] = jnp.concatenate([left_ref[w], left_ref[w]], axis=1)
        rights[:, w * BLK : (w + 1) * BLK] = right_ref[w]
    pl.semaphore_wait(barrier, len(partners))

    def remote(src, dst, send, recv, to):
        return pltpu.make_async_remote_copy(
            src_ref=src, dst_ref=dst, send_sem=send, recv_sem=recv, device_id=to, device_id_type=MESH
        )

    def pair_copy(k):
        return remote(terms.at[k, 1 - core], pair.at[k], s0.at[k], r0.at[k], twin)

    def bank(k, carry):
        load(k).wait()
        for w in range(NWEIGHT):
            high, low = split(held[k * NWEIGHT + w])
            both = jnp.concatenate([high, low], axis=0).astype(BF16)
            one = jnp.dot(lefts[w], both, preferred_element_type=F32).astype(BF16)
            formed[0, :, w * BLK : (w + 1) * BLK] = one[:, 0:BLK]
            formed[1, :, w * BLK : (w + 1) * BLK] = one[:, BLK : 2 * BLK]
        for part in range(2):
            term = lax.dot_general(
                formed[part], rights[...], (((1,), (1,)), ((), ())), preferred_element_type=F32
            )
            for half in range(2):
                cut = term[:, half * BLK : (half + 1) * BLK].reshape((4, 2, 4, 8, BLK))
                for which in range(2):
                    terms[k, which, part, :, half * 4 : half * 4 + 4] = cut[:, which]
        pair_copy(k).start()
        return carry

    lax.fori_loop(0, BANKS, bank, 0)

    def add_pair(k, carry):
        pair_copy(k).wait_recv()
        bz = lax.div(k, 2)
        for part in range(2):
            by = lax.rem(k, 2) * 2 + part
            both = terms[k, core, part] + pair[k, part]
            parts[0][:, by, bz] = both[:, 0:3]
            parts[1][by, bz] = both[:, 3:6]
            parts[2][bz, :, by] = both[:, 6:8]
        return carry

    lax.fori_loop(0, BANKS, add_pair, 0)

    copies = []
    for o in range(3):
        axis = ORDERS[o][0]
        at = place[axis]
        plus, minus, opposite = (lax.rem(at + by, 4) for by in (1, 3, 2))
        to_plus, to_minus = along(axis, 1), along(axis, 3)
        low, high = slice(0, 2), slice(2, 4)
        part, relay, first = parts[o], relays[o], firsts[o]
        moves = (
            (part.at[opposite, low], relay.at[0], to_plus),
            (part.at[opposite, high], relay.at[1], to_minus),
            (part.at[plus, high], first.at[0, high], to_plus),
            (part.at[minus, low], first.at[1, low], to_minus),
            (part.at[plus, low], first.at[0, low], to_plus),
            (part.at[minus, high], first.at[1, high], to_minus),
        )
        copies.append([remote(src, dst, s1.at[o, n], r1.at[o, n], to) for n, (src, dst, to) in enumerate(moves)])
    for pick in ((0, 1), (2, 3)):
        for o in range(3):
            for n in pick:
                copies[o][n].start()
    for o in range(3):
        at = place[ORDERS[o][0]]
        plus, minus = lax.rem(at + 1, 4), lax.rem(at + 3, 4)
        copies[o][0].wait_recv()
        parts[o][plus, 0:2] += relays[o][0]
        copies[o][4].start()
        copies[o][1].wait_recv()
        parts[o][minus, 2:4] += relays[o][1]
        copies[o][5].start()

    def exchange(source, slots, axis, send, recv):
        at = place[axis]
        made = []
        for n, by in enumerate((1, 3, 2)):
            made.append(
                remote(source.at[lax.rem(at + by, 4)], slots.at[n], send.at[n], recv.at[n], along(axis, by))
            )
        for copy in made:
            copy.start()
        return made

    later = []
    for o in range(3):
        for n in range(2, 6):
            copies[o][n].wait_recv()
        owns1[o][...] = parts[o][place[ORDERS[o][0]]] + firsts[o][0] + firsts[o][1]
        later.append(exchange(owns1[o], seconds[o], ORDERS[o][1], s2.at[o], r2.at[o]))
    last = []
    for o in range(3):
        for copy in later[o]:
            copy.wait_recv()
        slots = seconds[o]
        owns2[o][...] = owns1[o][place[ORDERS[o][1]]] + slots[0] + slots[1] + slots[2]
        last.append(exchange(owns2[o], thirds[o], ORDERS[o][2], s3.at[o], r3.at[o]))
    for o in range(3):
        for copy in last[o]:
            copy.wait_recv()
        slots = thirds[o]
        share[tm, TILES[o][0] : TILES[o][1]] = owns2[o][place[ORDERS[o][2]]] + slots[0] + slots[1] + slots[2]

    gathers = [
        remote(share.at[tm], share.at[tm], s4.at[n], r4.at[n], to) for n, to in enumerate((twin, side, cross))
    ]
    for copy in gathers:
        copy.start()
    for k in range(BANKS):
        pair_copy(k).wait_send()
    for group in copies + later + last:
        for copy in group:
            copy.wait_send()
    for copy in gathers:
        copy.wait_recv()
    for t in range(TMS):
        for half in range(2):
            for r in range(4):
                rows = slice(t * 32 + r * 8, t * 32 + r * 8 + 8)
                out_ref[rows, half * BLK : (half + 1) * BLK] = share[t, half * 4 + r]
    for copy in gathers:
        copy.wait_send()


def beam_banks(left, right, sums):
    tile = (8, BLK)
    vmem = lambda *dims: pltpu.VMEM(dims + tile, F32)
    dma = lambda *dims: pltpu.SemaphoreType.DMA(dims)
    scratch = [
        pltpu.VMEM((BANKS * NWEIGHT, BLK, 2 * BLK), F32),
        pltpu.VMEM((NWEIGHT, BEAMS, 2 * BLK), BF16),
        pltpu.VMEM((BEAMS, NWEIGHT * BLK), BF16),
        pltpu.VMEM((2, BEAMS, NWEIGHT * BLK), BF16),
        vmem(BANKS, 2, 2, 4, 8),
        vmem(BANKS, 2, 4, 8),
    ]
    scratch += [vmem(4, 4, 4, n) for n in COUNTS]
    scratch += [vmem(2, 2, 4, n) for n in COUNTS]
    scratch += [vmem(2, 4, 4, n) for n in COUNTS]
    scratch += [vmem(4, 4, n) for n in COUNTS]
    scratch += [vmem(3, 4, n) for n in COUNTS]
    scratch += [vmem(4, n) for n in COUNTS]
    scratch += [vmem(3, n) for n in COUNTS]
    scratch += [vmem(TMS, 8)]
    scratch += [dma(BANKS), dma(BANKS), dma(BANKS), dma(3, 6), dma(3, 6)]
    scratch += [dma(3, 3), dma(3, 3), dma(3, 3), dma(3, 3), dma(3), dma(3)]
    return pl.pallas_call(
        beams_kernel,
        in_specs=[
            pl.BlockSpec(memory_space=pltpu.VMEM),
            pl.BlockSpec(memory_space=pltpu.VMEM),
            pl.BlockSpec(memory_space=pl.ANY),
        ],
        out_specs=pl.BlockSpec(memory_space=pltpu.VMEM),
        out_shape=jax.ShapeDtypeStruct((BLK, BEAMS), F32),
        scratch_shapes=scratch,
        compiler_params=pltpu.CompilerParams(
            collective_id=1, has_side_effects=True, vmem_limit_bytes=48 * MIB
        ),
        name="beams",
    )(left, right, sums)


def local(visibilities, model, beam_left, beam_right, weight_index, target_bank, widths):
    vis = visibilities.reshape((MATS, 2, N, N))
    mod = model.reshape((MATS, 2, N, N))
    referenced = referenced_gains(vis, mod)
    inverse = inverse_gains(referenced, widths)
    sums = calibrated_sums(weight_index, target_bank.reshape((MATS, 16)), inverse, vis)
    return beam_banks(beam_left, beam_right, sums)


def solution(mesh):
    return jax.shard_map(
        local,
        mesh=mesh,
        in_specs=(
            P("chan", "tm", None, None, None),
            P("chan", "tm", None, None, None),
            P(),
            P(),
            P("chan", None),
            P("chan", "tm", None),
            P("chan"),
        ),
        out_specs=P("chan", None),
        check_vma=False,
    )
```

```python
import jax
import jax.numpy as jnp
from jax import lax
from jax.experimental import pallas as pl
from jax.experimental.pallas import tpu as pltpu
from jax.sharding import PartitionSpec as P

N = 512
BLK = 128
BEAMS = 256
BANKS = 8
NWEIGHT = 8
ITERS = 6
HW = 2
LC = 2
LT = 4
TMS = 4
ALL_T = 16
MATS = LC * LT
MESH = pl.DeviceIdType.MESH
MIB = 1024 * 1024
F32 = jnp.float32
BF16 = jnp.bfloat16

epsilon = 1e-06


def split(x):
    high = x.astype(BF16).astype(F32)
    return high, x - high


def gains_kernel(
    width_hbm, vis_hbm, mod_hbm, inv_ref, vis_ref,
    mod, cross, power, mine, halo, width, load_sem, width_sem, send_sem, recv_sem,
):
    me = lax.axis_index("tm")
    chan = lax.axis_index("chan")
    right = (chan, lax.rem(me + 1, TMS))
    left = (chan, lax.rem(me + TMS - 1, TMS))
    barrier = pltpu.get_barrier_semaphore()
    for other in (left, right):
        pl.semaphore_signal(barrier, inc=1, device_id=other, device_id_type=MESH)

    def load(m):
        return (
            pltpu.make_async_copy(vis_hbm.at[m], vis_ref.at[m], load_sem.at[0, m]),
            pltpu.make_async_copy(mod_hbm.at[m], mod.at[m], load_sem.at[1, m]),
        )

    for m in range(MATS):
        for copy in load(m):
            copy.start()
    width_copy = pltpu.make_async_copy(width_hbm, width, width_sem)
    width_copy.start()

    row = lax.broadcasted_iota(jnp.int32, (MATS, N), 0)
    strip = 32

    def form(m, sums):
        for copy in load(m):
            copy.wait()
        totals = [jnp.zeros((8, N), F32) for _ in range(3)]
        for top in range(0, N, strip):
            rows = slice(top, top + strip)
            vis_re = vis_ref[m, 0, rows, :].astype(F32)
            vis_im = vis_ref[m, 1, rows, :].astype(F32)
            mod_re = mod[m, 0, rows, :].astype(F32)
            mod_im = mod[m, 1, rows, :].astype(F32)
            cross_re = mod_re * vis_re + mod_im * vis_im
            cross_im = mod_im * vis_re - mod_re * vis_im
            size = mod_re * mod_re + mod_im * mod_im
            cross[m, 0, rows, :] = cross_re.astype(BF16)
            cross[m, 1, rows, :] = cross_im.astype(BF16)
            power[m, rows, :] = size
            for n, one in enumerate((cross_re, cross_im, size)):
                totals[n] = totals[n] + jnp.sum(one.reshape((strip // 8, 8, N)), axis=0)
        here = row == m
        return tuple(
            jnp.where(here, jnp.sum(total, axis=0, keepdims=True), old) for total, old in zip(totals, sums)
        )

    zeros = jnp.zeros((MATS, N), F32)
    num_re, num_im, den = lax.fori_loop(0, MATS, form, (zeros, zeros, zeros))
    den = den + epsilon

    def sweep(k, gains):
        gain_re, gain_im = gains
        size = gain_re * gain_re + gain_im * gain_im
        by_row = jnp.transpose(size)
        both = jnp.concatenate([*split(gain_re), *split(gain_im)], axis=0).astype(BF16)
        num_re, num_im, den = zeros, zeros, zeros
        for m in range(MATS):
            with_re = jnp.dot(both, cross[m, 0], preferred_element_type=F32)
            with_im = jnp.dot(both, cross[m, 1], preferred_element_type=F32)
            one_re = (with_re[0:8] + with_re[8:16]) - (with_im[16:24] + with_im[24:32])
            one_im = (with_im[0:8] + with_im[8:16]) + (with_re[16:24] + with_re[24:32])
            total = jnp.zeros((8, N), F32)
            for top in range(0, N, strip):
                rows = slice(top, top + strip)
                total = total + jnp.sum((by_row[rows, m : m + 1] * power[m, rows, :]).reshape((strip // 8, 8, N)), axis=0)
            here = row == m
            num_re = jnp.where(here, one_re, num_re)
            num_im = jnp.where(here, one_im, num_im)
            den = jnp.where(here, jnp.sum(total, axis=0, keepdims=True), den)
        den = den + epsilon
        new_re = num_re / den
        new_im = num_im / den
        odd = lax.rem(k, 2) == 1
        gain_re = jnp.where(odd, 0.5 * (new_re + gain_re), new_re)
        gain_im = jnp.where(odd, 0.5 * (new_im + gain_im), new_im)
        return gain_re, gain_im

    gain_re, gain_im = lax.fori_loop(1, ITERS, sweep, (num_re / den, num_im / den))
    first_re = gain_re[:, 0:1]
    first_im = gain_im[:, 0:1]
    divisor = jnp.maximum(jnp.sqrt(first_re * first_re + first_im * first_im), 1.0)
    unit_re = first_re / divisor
    unit_im = -first_im / divisor
    mine[0] = gain_re * unit_re - gain_im * unit_im
    mine[1] = gain_re * unit_im + gain_im * unit_re

    pl.semaphore_wait(barrier, 2)
    copies = [
        pltpu.make_async_remote_copy(
            src_ref=mine,
            dst_ref=halo.at[slot],
            send_sem=send_sem.at[slot],
            recv_sem=recv_sem.at[slot],
            device_id=other,
            device_id_type=MESH,
        )
        for slot, other in ((0, right), (1, left))
    ]
    for copy in copies:
        copy.start()
    width_copy.wait()
    within = lax.rem(row, LT)
    interval = me * LT + within
    half_width = jnp.where(row < LT, width[0], width[1])
    for copy in copies:
        copy.wait()

    def moved(x, offset):
        return x if offset % MATS == 0 else jnp.concatenate([x[offset % MATS :], x[: offset % MATS]], axis=0)

    sums = []
    for part in range(2):
        here = mine[part]
        before = halo[0, part]
        after = halo[1, part]
        total = jnp.zeros((MATS, N), F32)
        count = jnp.zeros((MATS, N), F32)
        for offset in range(-HW, HW + 1):
            value = moved(here, offset)
            if offset > 0:
                value = jnp.where(within + offset < LT, value, moved(after, offset - LT))
            if offset < 0:
                value = jnp.where(within + offset >= 0, value, moved(before, offset + LT))
            inside = (half_width >= abs(offset)) & (interval + offset >= 0) & (interval + offset < ALL_T)
            total = total + jnp.where(inside, value, 0.0)
            count = count + jnp.where(inside, 1.0, 0.0)
        sums.append(total / count)
    smooth_re, smooth_im = sums
    size = jnp.maximum(smooth_re * smooth_re + smooth_im * smooth_im, 1.0)
    inv_ref[0] = smooth_re / size
    inv_ref[1] = -smooth_im / size


def inverse_gains(widths, vis, mod):
    hbm = pl.BlockSpec(memory_space=pltpu.HBM)
    vmem = pl.BlockSpec(memory_space=pltpu.VMEM)
    return pl.pallas_call(
        gains_kernel,
        in_specs=[hbm, hbm, hbm],
        out_specs=[vmem, vmem],
        out_shape=[
            jax.ShapeDtypeStruct((2, MATS, N), F32),
            jax.ShapeDtypeStruct((MATS, 2, N, N), BF16),
        ],
        scratch_shapes=[
            pltpu.VMEM((MATS, 2, N, N), BF16),
            pltpu.VMEM((MATS, 2, N, N), BF16),
            pltpu.VMEM((MATS, N, N), F32),
            pltpu.VMEM((2, MATS, N), F32),
            pltpu.VMEM((2, 2, MATS, N), F32),
            pltpu.SMEM((LC,), jnp.int32),
            pltpu.SemaphoreType.DMA((2, MATS)),
            pltpu.SemaphoreType.DMA,
            pltpu.SemaphoreType.DMA((2,)),
            pltpu.SemaphoreType.DMA((2,)),
        ],
        compiler_params=pltpu.CompilerParams(
            collective_id=0, has_side_effects=True, vmem_limit_bytes=34 * MIB
        ),
        name="gains",
    )(*(pltpu.with_memory_space_constraint(x, pltpu.HBM) for x in (widths, vis, mod)))


def sums_kernel(weight_hbm, bank_hbm, inv_ref, vis_ref, out_ref, weight, bank, scale_a, scale_b, sem):
    copies = [
        pltpu.make_async_copy(weight_hbm, weight, sem.at[0]),
        pltpu.make_async_copy(bank_hbm, bank, sem.at[1]),
    ]
    for copy in copies:
        copy.start()
    row = lax.broadcasted_iota(jnp.int32, (16, N), 0)
    groups = N // BLK
    strip = 32

    def stacked(rows):
        out = jnp.zeros((16, N), F32)
        for k, one in enumerate(rows):
            out = jnp.where(row == k, one, out)
        return out.astype(BF16)

    def scales(m, scale):
        re_high, re_low = split(inv_ref[0, pl.ds(m, 1), :])
        im_high, im_low = split(inv_ref[1, pl.ds(m, 1), :])
        by_row_re = stacked([re_high, re_low, re_high, im_high, im_low, im_high])
        by_row_im = stacked([im_high, im_low, im_high, -re_high, -re_low, -re_high])
        by_col = stacked([re_high, re_high, re_low, im_high, im_high, im_low])
        depth_first = (((0,), (0,)), ((), ()))
        scale[0] = lax.dot_general(by_row_re, by_col, depth_first, preferred_element_type=F32)
        scale[1] = lax.dot_general(by_row_im, by_col, depth_first, preferred_element_type=F32)

    def add(m, c, scale):
        for i in range(groups):
            for j in range(groups):
                cols = slice(j * BLK, (j + 1) * BLK)
                place = bank[m, i * groups + j] * NWEIGHT + weight[c, i * groups + j]
                for s in range(0, BLK, strip):
                    rows = slice(i * BLK + s, i * BLK + s + strip)
                    to = slice(s, s + strip)
                    vis_re = vis_ref[m, 0, rows, cols].astype(F32)
                    vis_im = vis_ref[m, 1, rows, cols].astype(F32)
                    one_re = scale[0, rows, cols]
                    one_im = scale[1, rows, cols]
                    out_ref[place, to, 0:BLK] += one_re * vis_re - one_im * vis_im
                    out_ref[place, to, BLK : 2 * BLK] += one_re * vis_im + one_im * vis_re

    def clear(k, carry):
        out_ref[k] = jnp.zeros((BLK, 2 * BLK), F32)
        return carry

    scales(0, scale_a)
    lax.fori_loop(0, BANKS * NWEIGHT, clear, 0)
    for copy in copies:
        copy.wait()

    def two(q, carry):
        c = lax.div(q, LT // 2)
        scales(2 * q + 1, scale_b)
        add(2 * q, c, scale_a)
        scales(jnp.minimum(2 * q + 2, MATS - 1), scale_a)
        add(2 * q + 1, c, scale_b)
        return carry

    lax.fori_loop(0, MATS // 2, two, 0)


def calibrated_sums(weight_index, target_bank, inverse, vis):
    hbm = pl.BlockSpec(memory_space=pltpu.HBM)
    vmem = pl.BlockSpec(memory_space=pltpu.VMEM)
    return pl.pallas_call(
        sums_kernel,
        in_specs=[hbm, hbm, vmem, vmem],
        out_specs=vmem,
        out_shape=jax.ShapeDtypeStruct((BANKS * NWEIGHT, BLK, 2 * BLK), F32),
        scratch_shapes=[
            pltpu.SMEM((LC, 16), jnp.int32),
            pltpu.SMEM((MATS, 16), jnp.int32),
            pltpu.VMEM((2, N, N), F32),
            pltpu.VMEM((2, N, N), F32),
            pltpu.SemaphoreType.DMA((2,)),
        ],
        compiler_params=pltpu.CompilerParams(vmem_limit_bytes=12 * MIB),
        name="sums",
    )(*(pltpu.with_memory_space_constraint(x, pltpu.HBM) for x in (weight_index, target_bank)), inverse, vis)


ORDERS = (("x", "y", "z"), ("y", "z", "x"), ("z", "x", "y"))
TILES = ((0, 3), (3, 6), (6, 8))
COUNTS = tuple(high - low for low, high in TILES)


def beams_kernel(left_ref, right_ref, sums_ref, out_ref, *scratch):
    (lefts, rights, formed, terms, pair) = scratch[0:5]
    parts = scratch[5:8]
    relays = scratch[8:11]
    firsts = scratch[11:14]
    owns1 = scratch[14:17]
    seconds = scratch[17:20]
    owns2 = scratch[20:23]
    thirds = scratch[23:26]
    share = scratch[26]
    (s0, r0, s1, r1, s2, r2, s3, r3, s4, r4) = scratch[27:37]

    chan = lax.axis_index("chan")
    tm = lax.axis_index("tm")
    z = lax.div(chan, 8)
    y = lax.rem(lax.div(chan, 2), 4)
    x_low = lax.div(tm, 2)
    x = lax.rem(chan, 2) * 2 + x_low
    core = lax.rem(tm, 2)
    place = {"x": x, "y": y, "z": z}

    def device(at, which=core):
        return (
            (at["z"] * 4 + at["y"]) * 2 + lax.div(at["x"], 2),
            lax.rem(at["x"], 2) * 2 + which,
        )

    def along(axis, by):
        return device({**place, axis: lax.rem(place[axis] + by, 4)})

    twin = device(place, 1 - core)
    other_low = lax.div(x, 2) * 2 + (1 - x_low)
    side = device({**place, "x": other_low})
    cross = device({**place, "x": other_low}, 1 - core)

    barrier = pltpu.get_barrier_semaphore()
    partners = [twin, cross] + [along(axis, by) for axis in "xyz" for by in (1, 2, 3)]
    for other in partners:
        pl.semaphore_signal(barrier, inc=1, device_id=other, device_id_type=MESH)

    for w in range(NWEIGHT):
        lefts[w] = jnp.concatenate([left_ref[w], left_ref[w]], axis=1)
        rights[:, w * BLK : (w + 1) * BLK] = right_ref[w]
    pl.semaphore_wait(barrier, len(partners))

    def remote(src, dst, send, recv, to):
        return pltpu.make_async_remote_copy(
            src_ref=src, dst_ref=dst, send_sem=send, recv_sem=recv, device_id=to, device_id_type=MESH
        )

    def pair_copy(k):
        return remote(terms.at[k, 1 - core], pair.at[k], s0.at[k], r0.at[k], twin)

    def bank(k, carry):
        for w in range(NWEIGHT):
            high, low = split(sums_ref[k * NWEIGHT + w])
            both = jnp.concatenate([high, low], axis=0).astype(BF16)
            one = jnp.dot(lefts[w], both, preferred_element_type=F32).astype(BF16)
            formed[0, :, w * BLK : (w + 1) * BLK] = one[:, 0:BLK]
            formed[1, :, w * BLK : (w + 1) * BLK] = one[:, BLK : 2 * BLK]
        for part in range(2):
            term = lax.dot_general(
                formed[part], rights[...], (((1,), (1,)), ((), ())), preferred_element_type=F32
            )
            for half in range(2):
                cut = term[:, half * BLK : (half + 1) * BLK].reshape((4, 2, 4, 8, BLK))
                for which in range(2):
                    terms[k, which, part, :, half * 4 : half * 4 + 4] = cut[:, which]
        pair_copy(k).start()
        return carry

    lax.fori_loop(0, BANKS, bank, 0)

    def add_pair(k, carry):
        pair_copy(k).wait_recv()
        bz = lax.div(k, 2)
        for part in range(2):
            by = lax.rem(k, 2) * 2 + part
            both = terms[k, core, part] + pair[k, part]
            parts[0][:, by, bz] = both[:, 0:3]
            parts[1][by, bz] = both[:, 3:6]
            parts[2][bz, :, by] = both[:, 6:8]
        return carry

    lax.fori_loop(0, BANKS, add_pair, 0)

    copies = []
    for o in range(3):
        axis = ORDERS[o][0]
        at = place[axis]
        plus, minus, opposite = (lax.rem(at + by, 4) for by in (1, 3, 2))
        to_plus, to_minus = along(axis, 1), along(axis, 3)
        low, high = slice(0, 2), slice(2, 4)
        part, relay, first = parts[o], relays[o], firsts[o]
        moves = (
            (part.at[opposite, low], relay.at[0], to_plus),
            (part.at[opposite, high], relay.at[1], to_minus),
            (part.at[plus, high], first.at[0, high], to_plus),
            (part.at[minus, low], first.at[1, low], to_minus),
            (part.at[plus, low], first.at[0, low], to_plus),
            (part.at[minus, high], first.at[1, high], to_minus),
        )
        copies.append([remote(src, dst, s1.at[o, n], r1.at[o, n], to) for n, (src, dst, to) in enumerate(moves)])
    for pick in ((0, 1), (2, 3)):
        for o in range(3):
            for n in pick:
                copies[o][n].start()
    for o in range(3):
        at = place[ORDERS[o][0]]
        plus, minus = lax.rem(at + 1, 4), lax.rem(at + 3, 4)
        copies[o][0].wait_recv()
        parts[o][plus, 0:2] += relays[o][0]
        copies[o][4].start()
        copies[o][1].wait_recv()
        parts[o][minus, 2:4] += relays[o][1]
        copies[o][5].start()

    def exchange(source, slots, axis, send, recv):
        at = place[axis]
        made = []
        for n, by in enumerate((1, 3, 2)):
            made.append(
                remote(source.at[lax.rem(at + by, 4)], slots.at[n], send.at[n], recv.at[n], along(axis, by))
            )
        for copy in made:
            copy.start()
        return made

    later = []
    for o in range(3):
        for n in range(2, 6):
            copies[o][n].wait_recv()
        owns1[o][...] = parts[o][place[ORDERS[o][0]]] + firsts[o][0] + firsts[o][1]
        later.append(exchange(owns1[o], seconds[o], ORDERS[o][1], s2.at[o], r2.at[o]))
    last = []
    for o in range(3):
        for copy in later[o]:
            copy.wait_recv()
        slots = seconds[o]
        owns2[o][...] = owns1[o][place[ORDERS[o][1]]] + slots[0] + slots[1] + slots[2]
        last.append(exchange(owns2[o], thirds[o], ORDERS[o][2], s3.at[o], r3.at[o]))
    for o in range(3):
        for copy in last[o]:
            copy.wait_recv()
        slots = thirds[o]
        share[tm, TILES[o][0] : TILES[o][1]] = owns2[o][place[ORDERS[o][2]]] + slots[0] + slots[1] + slots[2]

    gathers = [
        remote(share.at[tm], share.at[tm], s4.at[n], r4.at[n], to) for n, to in enumerate((twin, side, cross))
    ]
    for copy in gathers:
        copy.start()
    for k in range(BANKS):
        pair_copy(k).wait_send()
    for group in copies + later + last:
        for copy in group:
            copy.wait_send()
    for copy in gathers:
        copy.wait_recv()
    for t in range(TMS):
        for half in range(2):
            for r in range(4):
                rows = slice(t * 32 + r * 8, t * 32 + r * 8 + 8)
                out_ref[rows, half * BLK : (half + 1) * BLK] = share[t, half * 4 + r]
    for copy in gathers:
        copy.wait_send()


def beam_banks(left, right, sums):
    tile = (8, BLK)
    vmem = lambda *dims: pltpu.VMEM(dims + tile, F32)
    dma = lambda *dims: pltpu.SemaphoreType.DMA(dims)
    scratch = [
        pltpu.VMEM((NWEIGHT, BEAMS, 2 * BLK), BF16),
        pltpu.VMEM((BEAMS, NWEIGHT * BLK), BF16),
        pltpu.VMEM((2, BEAMS, NWEIGHT * BLK), BF16),
        vmem(BANKS, 2, 2, 4, 8),
        vmem(BANKS, 2, 4, 8),
    ]
    scratch += [vmem(4, 4, 4, n) for n in COUNTS]
    scratch += [vmem(2, 2, 4, n) for n in COUNTS]
    scratch += [vmem(2, 4, 4, n) for n in COUNTS]
    scratch += [vmem(4, 4, n) for n in COUNTS]
    scratch += [vmem(3, 4, n) for n in COUNTS]
    scratch += [vmem(4, n) for n in COUNTS]
    scratch += [vmem(3, n) for n in COUNTS]
    scratch += [vmem(TMS, 8)]
    scratch += [dma(BANKS), dma(BANKS), dma(3, 6), dma(3, 6)]
    scratch += [dma(3, 3), dma(3, 3), dma(3, 3), dma(3, 3), dma(3), dma(3)]
    return pl.pallas_call(
        beams_kernel,
        in_specs=[
            pl.BlockSpec(memory_space=pltpu.VMEM),
            pl.BlockSpec(memory_space=pltpu.VMEM),
            pl.BlockSpec(memory_space=pltpu.VMEM),
        ],
        out_specs=pl.BlockSpec(memory_space=pltpu.VMEM),
        out_shape=jax.ShapeDtypeStruct((BLK, BEAMS), F32),
        scratch_shapes=scratch,
        compiler_params=pltpu.CompilerParams(
            collective_id=1, has_side_effects=True, vmem_limit_bytes=24 * MIB
        ),
        name="beams",
    )(left, right, sums)


def local(visibilities, model, beam_left, beam_right, weight_index, target_bank, widths):
    vis = visibilities.reshape((MATS, 2, N, N))
    mod = model.reshape((MATS, 2, N, N))
    inverse, vis = inverse_gains(widths, vis, mod)
    sums = calibrated_sums(weight_index, target_bank.reshape((MATS, 16)), inverse, vis)
    return beam_banks(beam_left, beam_right, sums)


def solution(mesh):
    return jax.shard_map(
        local,
        mesh=mesh,
        in_specs=(
            P("chan", "tm", None, None, None),
            P("chan", "tm", None, None, None),
            P(),
            P(),
            P("chan", None),
            P("chan", "tm", None),
            P("chan"),
        ),
        out_specs=P("chan", None),
        check_vma=False,
    )
```

```python
import functools

import jax
import jax.numpy as jnp
from jax import lax
from jax.experimental import pallas as pl
from jax.experimental.pallas import tpu as pltpu
from jax.sharding import PartitionSpec as P

N = 512
BLK = 128
BEAMS = 256
BANKS = 8
NWEIGHT = 8
ITERS = 6
HW = 2
LC = 2
LT = 4
TMS = 4
ALL_T = 16
MATS = LC * LT
MESH = pl.DeviceIdType.MESH
MIB = 1024 * 1024
F32 = jnp.float32
BF16 = jnp.bfloat16

epsilon = 1e-06


def split(x):
    high = x.astype(BF16).astype(F32)
    return high, x - high


def gains_kernel(
    width_hbm, vis_hbm, mod_hbm, inv_ref, vis_ref,
    mod, cross_0, cross_1, power_0, power_1, sums_1, mine, halo, width, load_sem, width_sem, send_sem, recv_sem,
):
    me = lax.axis_index("tm")
    chan = lax.axis_index("chan")
    right = (chan, lax.rem(me + 1, TMS))
    left = (chan, lax.rem(me + TMS - 1, TMS))
    barrier = pltpu.get_barrier_semaphore()
    for other in (left, right):
        pl.semaphore_signal(barrier, inc=1, device_id=other, device_id_type=MESH)

    def load(m):
        return (
            pltpu.make_async_copy(vis_hbm.at[m], vis_ref.at[m], load_sem.at[0, m]),
            pltpu.make_async_copy(mod_hbm.at[m], mod.at[m], load_sem.at[1, m]),
        )

    for m in range(MATS):
        for copy in load(m):
            copy.start()
    width_copy = pltpu.make_async_copy(width_hbm, width, width_sem)
    width_copy.start()

    row = lax.broadcasted_iota(jnp.int32, (MATS, N), 0)
    zeros = jnp.zeros((MATS, N), F32)
    strip = 32
    strips = N // strip

    def form(m, slot, top, cross, power):
        rows = pl.ds(top, strip)
        vis_re = vis_ref[m, 0, rows, :].astype(F32)
        vis_im = vis_ref[m, 1, rows, :].astype(F32)
        mod_re = mod[m, 0, rows, :].astype(F32)
        mod_im = mod[m, 1, rows, :].astype(F32)
        cross_re = mod_re * vis_re + mod_im * vis_im
        cross_im = mod_im * vis_re - mod_re * vis_im
        size = mod_re * mod_re + mod_im * mod_im
        cross[slot, 0, rows, :] = cross_re.astype(BF16)
        cross[slot, 1, rows, :] = cross_im.astype(BF16)
        power[slot, rows, :] = size
        return [jnp.sum(one.reshape((strip // 8, 8, N)), axis=0) for one in (cross_re, cross_im, size)]

    def spread(totals, sums, m):
        here = row == m
        return tuple(
            jnp.where(here, jnp.sum(total, axis=0, keepdims=True), old) for total, old in zip(totals, sums)
        )

    def form_whole(m, sums):
        for copy in load(m):
            copy.wait()
        totals = [jnp.zeros((8, N), F32) for _ in range(3)]
        for top in range(0, N, strip):
            totals = [old + new for old, new in zip(totals, form(m, m, top, cross_0, power_0))]
        return spread(totals, sums, m)

    def sweep(k, gains, first, cross, power):
        gain_re, gain_im = gains
        size = gain_re * gain_re + gain_im * gain_im
        by_row = jnp.transpose(size)
        both = jnp.concatenate([*split(gain_re), *split(gain_im)], axis=0).astype(BF16)
        num_re, num_im, den = zeros, zeros, zeros
        for m in range(LT):
            with_re = jnp.dot(both, cross[m, 0], preferred_element_type=F32)
            with_im = jnp.dot(both, cross[m, 1], preferred_element_type=F32)
            one_re = (with_re[0:8] + with_re[8:16]) - (with_im[16:24] + with_im[24:32])
            one_im = (with_im[0:8] + with_im[8:16]) + (with_re[16:24] + with_re[24:32])
            total = jnp.zeros((8, N), F32)
            for top in range(0, N, strip):
                rows = slice(top, top + strip)
                by = by_row[rows, first + m : first + m + 1]
                total = total + jnp.sum((by * power[m, rows, :]).reshape((strip // 8, 8, N)), axis=0)
            here = row == first + m
            num_re = jnp.where(here, one_re, num_re)
            num_im = jnp.where(here, one_im, num_im)
            den = jnp.where(here, jnp.sum(total, axis=0, keepdims=True), den)
        den = den + epsilon
        new_re = num_re / den
        new_im = num_im / den
        odd = lax.rem(k, 2) == 1
        new_re = jnp.where(odd, 0.5 * (new_re + gain_re), new_re)
        new_im = jnp.where(odd, 0.5 * (new_im + gain_im), new_im)
        mine = (row >= first) & (row < first + LT)
        return jnp.where(mine, new_re, gain_re), jnp.where(mine, new_im, gain_im)

    num_re, num_im, den = lax.fori_loop(0, LT, form_whole, (zeros, zeros, zeros))
    den = den + epsilon
    sums_1[...] = jnp.zeros_like(sums_1)
    units = -(-LT * strips // (ITERS - 1))

    def beside(k, gains):
        @pl.when(k <= LT)
        def _():
            for copy in load(LT + k - 1):
                copy.wait()

        new = sweep(k, gains, 0, cross_0, power_0)
        for i in range(units):
            unit = (k - 1) * units + i
            real = unit < LT * strips
            unit = jnp.minimum(unit, LT * strips - 1)
            slot = lax.div(unit, strips)
            top = pl.multiple_of(lax.rem(unit, strips) * strip, strip)
            for n, total in enumerate(form(LT + slot, slot, top, cross_1, power_1)):
                sums_1[slot, n] += jnp.where(real, total, 0.0)
        return new

    gains = lax.fori_loop(1, ITERS, beside, (num_re / den, num_im / den))
    sums = (zeros, zeros, zeros)
    for m in range(LT):
        sums = spread([sums_1[m, n] for n in range(3)], sums, LT + m)
    num_re, num_im, den = sums
    den = den + epsilon
    later = row >= LT
    gains = (jnp.where(later, num_re / den, gains[0]), jnp.where(later, num_im / den, gains[1]))
    gain_re, gain_im = lax.fori_loop(1, ITERS, lambda k, gains: sweep(k, gains, LT, cross_1, power_1), gains)
    first_re = gain_re[:, 0:1]
    first_im = gain_im[:, 0:1]
    divisor = jnp.maximum(jnp.sqrt(first_re * first_re + first_im * first_im), 1.0)
    unit_re = first_re / divisor
    unit_im = -first_im / divisor
    mine[0] = gain_re * unit_re - gain_im * unit_im
    mine[1] = gain_re * unit_im + gain_im * unit_re

    pl.semaphore_wait(barrier, 2)
    copies = [
        pltpu.make_async_remote_copy(
            src_ref=mine,
            dst_ref=halo.at[slot],
            send_sem=send_sem.at[slot],
            recv_sem=recv_sem.at[slot],
            device_id=other,
            device_id_type=MESH,
        )
        for slot, other in ((0, right), (1, left))
    ]
    for copy in copies:
        copy.start()
    width_copy.wait()
    within = lax.rem(row, LT)
    interval = me * LT + within
    half_width = jnp.where(row < LT, width[0], width[1])
    for copy in copies:
        copy.wait()

    def moved(x, offset):
        return x if offset % MATS == 0 else jnp.concatenate([x[offset % MATS :], x[: offset % MATS]], axis=0)

    sums = []
    for part in range(2):
        here = mine[part]
        before = halo[0, part]
        after = halo[1, part]
        total = jnp.zeros((MATS, N), F32)
        count = jnp.zeros((MATS, N), F32)
        for offset in range(-HW, HW + 1):
            value = moved(here, offset)
            if offset > 0:
                value = jnp.where(within + offset < LT, value, moved(after, offset - LT))
            if offset < 0:
                value = jnp.where(within + offset >= 0, value, moved(before, offset + LT))
            inside = (half_width >= abs(offset)) & (interval + offset >= 0) & (interval + offset < ALL_T)
            total = total + jnp.where(inside, value, 0.0)
            count = count + jnp.where(inside, 1.0, 0.0)
        sums.append(total / count)
    smooth_re, smooth_im = sums
    size = jnp.maximum(smooth_re * smooth_re + smooth_im * smooth_im, 1.0)
    inv_ref[0] = smooth_re / size
    inv_ref[1] = -smooth_im / size


def inverse_gains(widths, vis, mod):
    hbm = pl.BlockSpec(memory_space=pltpu.HBM)
    vmem = pl.BlockSpec(memory_space=pltpu.VMEM)
    return pl.pallas_call(
        gains_kernel,
        in_specs=[hbm, hbm, hbm],
        out_specs=[vmem, vmem],
        out_shape=[
            jax.ShapeDtypeStruct((2, MATS, N), F32),
            jax.ShapeDtypeStruct((MATS, 2, N, N), BF16),
        ],
        scratch_shapes=[
            pltpu.VMEM((MATS, 2, N, N), BF16),
            pltpu.VMEM((LT, 2, N, N), BF16),
            pltpu.VMEM((LT, 2, N, N), BF16),
            pltpu.VMEM((LT, N, N), F32),
            pltpu.VMEM((LT, N, N), F32),
            pltpu.VMEM((LT, 3, 8, N), F32),
            pltpu.VMEM((2, MATS, N), F32),
            pltpu.VMEM((2, 2, MATS, N), F32),
            pltpu.SMEM((LC,), jnp.int32),
            pltpu.SemaphoreType.DMA((2, MATS)),
            pltpu.SemaphoreType.DMA,
            pltpu.SemaphoreType.DMA((2,)),
            pltpu.SemaphoreType.DMA((2,)),
        ],
        compiler_params=pltpu.CompilerParams(
            collective_id=0, has_side_effects=True, vmem_limit_bytes=34 * MIB
        ),
        name="gains",
    )(*(pltpu.with_memory_space_constraint(x, pltpu.HBM) for x in (widths, vis, mod)))


def sums_kernel(weight_hbm, bank_hbm, inv_ref, vis_ref, out_ref, weight, bank, row_a, row_b, col_a, col_b, sem):
    copies = [
        pltpu.make_async_copy(weight_hbm, weight, sem.at[0]),
        pltpu.make_async_copy(bank_hbm, bank, sem.at[1]),
    ]
    for copy in copies:
        copy.start()
    row = lax.broadcasted_iota(jnp.int32, (16, N), 0)
    groups = N // BLK
    strip = 32

    def stacked(rows):
        out = jnp.zeros((16, N), F32)
        for k, one in enumerate(rows):
            out = jnp.where(row == k, one, out)
        return out

    def factors(m, by_row, by_col):
        re_high, re_low = split(inv_ref[0, pl.ds(m, 1), :])
        im_high, im_low = split(inv_ref[1, pl.ds(m, 1), :])
        by_row[...] = jnp.transpose(stacked([re_high, re_low, re_high, im_high, im_low, im_high])).astype(BF16)
        col_re = stacked([re_high, re_high, re_low, im_high, im_high, im_low]).astype(BF16)
        col_im = stacked([-im_high, -im_high, -im_low, re_high, re_high, re_low]).astype(BF16)
        for j in range(groups):
            cols = slice(j * BLK, (j + 1) * BLK)
            by_col[j, :, 0:BLK] = col_re[:, cols]
            by_col[j, :, BLK : 2 * BLK] = col_im[:, cols]

    def add(m, c, by_row, by_col):
        for j in range(groups):
            cols = slice(j * BLK, (j + 1) * BLK)
            for i in range(groups):
                place = bank[m, i * groups + j] * NWEIGHT + weight[c, i * groups + j]
                scale = jnp.dot(by_row[i * BLK : (i + 1) * BLK, :], by_col[j], preferred_element_type=F32)
                for s in range(0, BLK, strip):
                    rows = slice(i * BLK + s, i * BLK + s + strip)
                    to = slice(s, s + strip)
                    vis_re = vis_ref[m, 0, rows, cols].astype(F32)
                    vis_im = vis_ref[m, 1, rows, cols].astype(F32)
                    one_re = scale[to, 0:BLK]
                    one_im = scale[to, BLK : 2 * BLK]
                    out_ref[place, to, 0:BLK] += one_re * vis_re - one_im * vis_im
                    out_ref[place, to, BLK : 2 * BLK] += one_re * vis_im + one_im * vis_re

    def clear(k, carry):
        out_ref[k] = jnp.zeros((BLK, 2 * BLK), F32)
        return carry

    factors(0, row_a, col_a)
    lax.fori_loop(0, BANKS * NWEIGHT, clear, 0)
    for copy in copies:
        copy.wait()

    def two(q, carry):
        c = lax.div(q, LT // 2)
        factors(2 * q + 1, row_b, col_b)
        add(2 * q, c, row_a, col_a)
        factors(jnp.minimum(2 * q + 2, MATS - 1), row_a, col_a)
        add(2 * q + 1, c, row_b, col_b)
        return carry

    lax.fori_loop(0, MATS // 2, two, 0)


def calibrated_sums(weight_index, target_bank, inverse, vis):
    hbm = pl.BlockSpec(memory_space=pltpu.HBM)
    vmem = pl.BlockSpec(memory_space=pltpu.VMEM)
    return pl.pallas_call(
        sums_kernel,
        in_specs=[hbm, hbm, vmem, vmem],
        out_specs=vmem,
        out_shape=jax.ShapeDtypeStruct((BANKS * NWEIGHT, BLK, 2 * BLK), F32),
        scratch_shapes=[
            pltpu.SMEM((LC, 16), jnp.int32),
            pltpu.SMEM((MATS, 16), jnp.int32),
            pltpu.VMEM((N, 16), BF16),
            pltpu.VMEM((N, 16), BF16),
            pltpu.VMEM((N // BLK, 16, 2 * BLK), BF16),
            pltpu.VMEM((N // BLK, 16, 2 * BLK), BF16),
            pltpu.SemaphoreType.DMA((2,)),
        ],
        compiler_params=pltpu.CompilerParams(vmem_limit_bytes=12 * MIB),
        name="sums",
    )(*(pltpu.with_memory_space_constraint(x, pltpu.HBM) for x in (weight_index, target_bank)), inverse, vis)


STEPS = (2, 1, 3, 0)
A, B, C = slice(0, 3), slice(3, 6), slice(6, 8)


def beams_kernel(left_ref, right_ref, sums_ref, out_ref, *scratch):
    (lefts, rights, formed, terms, pair) = scratch[0:5]
    (parts_a, first_a, own1_a, second_a, own2_a, last_a) = scratch[5:11]
    (parts_b, first_b, own1_b, second_b, own2_b, last_b) = scratch[11:17]
    (parts_c, first_c, own1_c, second_c, own2_c, last_c) = scratch[17:23]
    share = scratch[23]
    sems = scratch[24:]
    (s_pair, s_a1, s_a2, s_a3, s_b1, s_b2, s_b3, s_c1, s_c2, s_c3, s_all) = sems[0:11]
    (r_pair, r_a1, r_a2, r_a3, r_b1, r_b2, r_b3, r_c1, r_c2, r_c3, r_all) = sems[11:22]

    chan = lax.axis_index("chan")
    tm = lax.axis_index("tm")
    z = lax.div(chan, 8)
    y = lax.rem(lax.div(chan, 2), 4)
    x_low = lax.div(tm, 2)
    x = lax.rem(chan, 2) * 2 + x_low
    core = lax.rem(tm, 2)
    place = {"x": x, "y": y, "z": z}

    def device(at, which=core):
        return (
            (at["z"] * 4 + at["y"]) * 2 + lax.div(at["x"], 2),
            lax.rem(at["x"], 2) * 2 + which,
        )

    def at(axis, by):
        return lax.rem(place[axis] + by, 4)

    near = {(axis, by): device({**place, axis: at(axis, by)}) for axis in "xyz" for by in (1, 2, 3)}
    twin = device(place, 1 - core)
    other_low = lax.div(x, 2) * 2 + (1 - x_low)
    side = device({**place, "x": other_low})
    cross = device({**place, "x": other_low}, 1 - core)

    barrier = pltpu.get_barrier_semaphore()
    partners = [twin, cross, *near.values()]
    for other in partners:
        pl.semaphore_signal(barrier, inc=1, device_id=other, device_id_type=MESH)

    for w in range(NWEIGHT):
        lefts[w] = jnp.concatenate([left_ref[w], left_ref[w]], axis=1)
        rights[:, w * BLK : (w + 1) * BLK] = right_ref[w]

    def remote(src, dst, send, recv, to):
        return pltpu.make_async_remote_copy(
            src_ref=src, dst_ref=dst, send_sem=send, recv_sem=recv, device_id=to, device_id_type=MESH
        )

    started = []

    def go(copies):
        for copy in copies:
            copy.start()
        started.extend(copies)

    def pair_copy(n):
        return remote(terms.at[n, 1 - core], pair.at[n], s_pair.at[n], r_pair.at[n], twin)

    def bank(n, step):
        k = at("z", STEPS[step]) * 2 + lax.rem(n, 2)
        for w in range(NWEIGHT):
            high, low = split(sums_ref[k * NWEIGHT + w])
            both = jnp.concatenate([high, low], axis=0).astype(BF16)
            one = jnp.dot(lefts[w], both, preferred_element_type=F32).astype(BF16)
            formed[0, :, w * BLK : (w + 1) * BLK] = one[:, 0:BLK]
            formed[1, :, w * BLK : (w + 1) * BLK] = one[:, BLK : 2 * BLK]
        for part in range(2):
            term = lax.dot_general(
                formed[part], rights[...], (((1,), (1,)), ((), ())), preferred_element_type=F32
            )
            for half in range(2):
                cut = term[:, half * BLK : (half + 1) * BLK].reshape((4, 2, 4, 8, BLK))
                for which in range(2):
                    terms[n, which, part, :, half * 4 : half * 4 + 4] = cut[:, which]

    def compute(step):
        def one(n, carry):
            bank(n, step)
            return carry

        lax.fori_loop(2 * step, 2 * step + 2, one, 0)
        if step == 0:
            pl.semaphore_wait(barrier, len(partners))
        for n in (2 * step, 2 * step + 1):
            pair_copy(n).start()

    def first_copies(step, axis, parts, first, send, recv):
        return [
            remote(
                parts.at[step, at(axis, by)], first.at[step, n], send.at[step, n], recv.at[step, n], near[axis, by]
            )
            for n, by in enumerate((2, 1, 3))
        ]

    @functools.cache
    def group_a(step):
        return first_copies(step, "x", parts_a, first_a, s_a1, r_a1)

    @functools.cache
    def group_b(step):
        return first_copies(step, "y", parts_b, first_b, s_b1, r_b1)

    @functools.cache
    def c1_copy(step):
        return along_z(step, parts_c, first_c, s_c1, r_c1)

    def pair_sum(step):
        for h in range(2):
            n = 2 * step + h
            pair_copy(n).wait_recv()
            for part in range(2):
                both = terms[n, core, part] + pair[n, part]
                row = 2 * h + part
                parts_a[step, :, row] = both[:, A]
                parts_b[step, row] = both[:, B]
                parts_c[step, :, row] = both[:, C]
        go(group_a(step) + group_b(step))
        if step != 3:
            go([c1_copy(step)])

    def spread(source, axis, slots, send, recv):
        return [
            remote(source.at[at(axis, by)], slots.at[n], send.at[n], recv.at[n], near[axis, by])
            for n, by in enumerate((2, 1, 3))
        ]

    def along_z(step, source, slots, send, recv):
        return remote(source.at[step], slots.at[step], send.at[step], recv.at[step], near["z", STEPS[step]])

    @functools.cache
    def a2_copy(step):
        return along_z(step, own1_a, second_a, s_a2, r_a2)

    @functools.cache
    def a3_copies():
        return spread(own2_a, "y", last_a, s_a3, r_a3)

    @functools.cache
    def b2_copy(step):
        return along_z(step, own1_b, second_b, s_b2, r_b2)

    @functools.cache
    def b3_copies():
        return spread(own2_b, "x", last_b, s_b3, r_b3)

    @functools.cache
    def c2_copies():
        return spread(own1_c, "x", second_c, s_c2, r_c2)

    @functools.cache
    def c3_copies():
        return spread(own2_c, "y", last_c, s_c3, r_c3)

    def arrived(copies):
        for copy in copies:
            copy.wait_recv()

    def finish_first(step):
        arrived(group_a(step))
        total = parts_a[step, x]
        for n in range(3):
            total = total + first_a[step, n]
        own1_a[step] = total
        if step != 3:
            go([a2_copy(step)])
        arrived(group_b(step))
        total = parts_b[step, y]
        for n in range(3):
            total = total + first_b[step, n]
        own1_b[step] = total
        if step != 3:
            go([b2_copy(step)])

    compute(0)
    compute(1)
    pair_sum(0)
    compute(2)
    pair_sum(1)
    compute(3)
    pair_sum(2)
    pair_sum(3)
    finish_first(0)
    finish_first(1)
    arrived([c1_copy(step) for step in range(3)])
    own1_c[...] = parts_c[3] + first_c[0] + first_c[1] + first_c[2]
    go(c2_copies())
    finish_first(2)
    finish_first(3)
    arrived([a2_copy(step) for step in range(3)])
    own2_a[...] = own1_a[3] + second_a[0] + second_a[1] + second_a[2]
    go(a3_copies())
    arrived([b2_copy(step) for step in range(3)])
    own2_b[...] = own1_b[3] + second_b[0] + second_b[1] + second_b[2]
    go(b3_copies())
    arrived(c2_copies())
    own2_c[...] = own1_c[x] + second_c[0] + second_c[1] + second_c[2]
    go(c3_copies())
    arrived(a3_copies())
    share[tm, A] = own2_a[y] + last_a[0] + last_a[1] + last_a[2]
    arrived(b3_copies())
    share[tm, B] = own2_b[x] + last_b[0] + last_b[1] + last_b[2]
    arrived(c3_copies())
    share[tm, C] = own2_c[y] + last_c[0] + last_c[1] + last_c[2]

    gathers = [
        remote(share.at[tm], share.at[tm], s_all.at[n], r_all.at[n], to) for n, to in enumerate((twin, side, cross))
    ]
    for copy in gathers:
        copy.start()
    for n in range(BANKS):
        pair_copy(n).wait_send()
    for copy in started:
        copy.wait_send()
    for copy in gathers:
        copy.wait_recv()
    for t in range(TMS):
        for half in range(2):
            for r in range(4):
                rows = slice(t * 32 + r * 8, t * 32 + r * 8 + 8)
                out_ref[rows, half * BLK : (half + 1) * BLK] = share[t, half * 4 + r]
    for copy in gathers:
        copy.wait_send()


def beam_banks(left, right, sums):
    tile = (8, BLK)
    vmem = lambda *dims: pltpu.VMEM(dims + tile, F32)
    dma = lambda *dims: pltpu.SemaphoreType.DMA(dims)
    scratch = [
        pltpu.VMEM((NWEIGHT, BEAMS, 2 * BLK), BF16),
        pltpu.VMEM((BEAMS, NWEIGHT * BLK), BF16),
        pltpu.VMEM((2, BEAMS, NWEIGHT * BLK), BF16),
        vmem(BANKS, 2, 2, 4, 8),
        vmem(BANKS, 2, 4, 8),
    ]
    scratch += [vmem(4, 4, 4, 3), vmem(4, 3, 4, 3), vmem(4, 4, 3), vmem(3, 4, 3), vmem(4, 3), vmem(3, 3)]
    scratch += [vmem(4, 4, 4, 3), vmem(4, 3, 4, 3), vmem(4, 4, 3), vmem(3, 4, 3), vmem(4, 3), vmem(3, 3)]
    scratch += [vmem(4, 4, 4, 2), vmem(3, 4, 4, 2), vmem(4, 4, 2), vmem(3, 4, 2), vmem(4, 2), vmem(3, 2)]
    scratch += [vmem(TMS, 8)]
    sems = [dma(BANKS), dma(4, 3), dma(3), dma(3), dma(4, 3), dma(3), dma(3), dma(3), dma(3), dma(3), dma(3)]
    return pl.pallas_call(
        beams_kernel,
        in_specs=[pl.BlockSpec(memory_space=pltpu.VMEM)] * 3,
        out_specs=pl.BlockSpec(memory_space=pltpu.VMEM),
        out_shape=jax.ShapeDtypeStruct((BLK, BEAMS), F32),
        scratch_shapes=scratch + sems + sems,
        compiler_params=pltpu.CompilerParams(
            collective_id=1, has_side_effects=True, vmem_limit_bytes=24 * MIB
        ),
        name="beams",
    )(left, right, sums)


def local(visibilities, model, beam_left, beam_right, weight_index, target_bank, widths):
    vis = visibilities.reshape((MATS, 2, N, N))
    mod = model.reshape((MATS, 2, N, N))
    inverse, vis = inverse_gains(widths, vis, mod)
    sums = calibrated_sums(weight_index, target_bank.reshape((MATS, 16)), inverse, vis)
    return beam_banks(beam_left, beam_right, sums)


def solution(mesh):
    return jax.shard_map(
        local,
        mesh=mesh,
        in_specs=(
            P("chan", "tm", None, None, None),
            P("chan", "tm", None, None, None),
            P(),
            P(),
            P("chan", None),
            P("chan", "tm", None),
            P("chan"),
        ),
        out_specs=P("chan", None),
        check_vma=False,
    )
```

```python
import functools

import jax
import jax.numpy as jnp
from jax import lax
from jax.experimental import pallas as pl
from jax.experimental.pallas import tpu as pltpu
from jax.sharding import PartitionSpec as P

N = 512
BLK = 128
BEAMS = 256
BANKS = 8
NWEIGHT = 8
ITERS = 6
HW = 2
LC = 2
LT = 4
TMS = 4
ALL_T = 16
MATS = LC * LT
MESH = pl.DeviceIdType.MESH
MIB = 1024 * 1024
F32 = jnp.float32
BF16 = jnp.bfloat16

epsilon = 1e-06


def split(x):
    high = x.astype(BF16).astype(F32)
    return high, x - high


def gains_kernel(
    width_hbm, vis_hbm, mod_hbm, inv_ref, vis_ref,
    mod, cross_0, cross_1, power_0, power_1, mine, halo, width, load_sem, width_sem, send_sem, recv_sem,
):
    me = lax.axis_index("tm")
    chan = lax.axis_index("chan")
    right = (chan, lax.rem(me + 1, TMS))
    left = (chan, lax.rem(me + TMS - 1, TMS))
    barrier = pltpu.get_barrier_semaphore()
    for other in (left, right):
        pl.semaphore_signal(barrier, inc=1, device_id=other, device_id_type=MESH)

    def load(m):
        return (
            pltpu.make_async_copy(vis_hbm.at[m], vis_ref.at[m], load_sem.at[0, m]),
            pltpu.make_async_copy(mod_hbm.at[m], mod.at[m], load_sem.at[1, m]),
        )

    for m in range(MATS):
        for copy in load(m):
            copy.start()
    width_copy = pltpu.make_async_copy(width_hbm, width, width_sem)
    width_copy.start()

    row = lax.broadcasted_iota(jnp.int32, (LT, N), 0)
    zeros = jnp.zeros((LT, N), F32)
    strip = 16
    strips = N // strip

    def form(m, slot, top, cross, power):
        rows = pl.ds(top, strip)
        vis_re = vis_ref[m, 0, rows, :].astype(F32)
        vis_im = vis_ref[m, 1, rows, :].astype(F32)
        mod_re = mod[m, 0, rows, :].astype(F32)
        mod_im = mod[m, 1, rows, :].astype(F32)
        cross_re = mod_re * vis_re + mod_im * vis_im
        cross_im = mod_im * vis_re - mod_re * vis_im
        size = mod_re * mod_re + mod_im * mod_im
        cross[slot, 0, rows, :] = cross_re.astype(BF16)
        cross[slot, 1, rows, :] = cross_im.astype(BF16)
        power[slot, rows, :] = size
        return [jnp.sum(one.reshape((strip // 8, 8, N)), axis=0) for one in (cross_re, cross_im, size)]

    def spread(totals, sums, slot):
        here = row == slot
        return tuple(
            jnp.where(here, jnp.sum(total, axis=0, keepdims=True), old) for total, old in zip(totals, sums)
        )

    def loaded(m):
        for copy in load(m):
            copy.wait()

    def form_whole(m, sums):
        loaded(m)
        totals = [jnp.zeros((8, N), F32) for _ in range(3)]
        for top in range(0, N, strip):
            totals = [old + new for old, new in zip(totals, form(m, m, top, cross_0, power_0))]
        return spread(totals, sums, m)

    def sweep(k, gains, cross, power, beside=lambda piece: None):
        gain_re, gain_im = gains
        size = gain_re * gain_re + gain_im * gain_im
        by_row = jnp.transpose(jnp.concatenate([size, size], axis=0))
        both = jnp.concatenate([*split(gain_re), *split(gain_im)], axis=0).astype(BF16)
        num_re, num_im, den = zeros, zeros, zeros
        for m in range(LT):
            halves = []
            for part in range(2):
                for half in range(2):
                    columns = cross[m, part, :, half * (N // 2) : (half + 1) * (N // 2)]
                    halves.append(jnp.dot(both, columns, preferred_element_type=F32))
                    beside(4 * m + 2 * part + half)
            with_re = jnp.concatenate(halves[0:2], axis=1)
            with_im = jnp.concatenate(halves[2:4], axis=1)
            one_re = (with_re[0:4] + with_re[4:8]) - (with_im[8:12] + with_im[12:16])
            one_im = (with_im[0:4] + with_im[4:8]) + (with_re[8:12] + with_re[12:16])
            total = jnp.zeros((8, N), F32)
            for top in range(0, N, strip):
                rows = slice(top, top + strip)
                total = total + jnp.sum((by_row[rows, m : m + 1] * power[m, rows, :]).reshape((strip // 8, 8, N)), axis=0)
            here = row == m
            num_re = jnp.where(here, one_re, num_re)
            num_im = jnp.where(here, one_im, num_im)
            den = jnp.where(here, jnp.sum(total, axis=0, keepdims=True), den)
        den = den + epsilon
        new_re = num_re / den
        new_im = num_im / den
        odd = lax.rem(k, 2) == 1
        return jnp.where(odd, 0.5 * (new_re + gain_re), new_re), jnp.where(odd, 0.5 * (new_im + gain_im), new_im)

    num_re, num_im, den = lax.fori_loop(0, LT, form_whole, (zeros, zeros, zeros))
    den = den + epsilon
    gains_0 = (num_re / den, num_im / den)
    sums = (zeros, zeros, zeros)
    totals = []
    pieces = (ITERS - 1) * LT * 4

    for k in range(1, ITERS):
        if k <= LT:
            loaded(LT + k - 1)

        def more(piece):
            nonlocal sums, totals
            piece += (k - 1) * LT * 4
            for unit in range(piece * LT * strips // pieces, (piece + 1) * LT * strips // pieces):
                slot, part = divmod(unit, strips)
                new = form(LT + slot, slot, part * strip, cross_1, power_1)
                totals = new if part == 0 else [old + one for old, one in zip(totals, new)]
                if part == strips - 1:
                    sums = spread(totals, sums, slot)

        gains_0 = sweep(k, gains_0, cross_0, power_0, more)

    num_re, num_im, den = sums
    den = den + epsilon
    gains_1 = lax.fori_loop(
        1, ITERS, lambda k, gains: sweep(k, gains, cross_1, power_1), (num_re / den, num_im / den)
    )
    gain_re, gain_im = (jnp.concatenate(pair, axis=0) for pair in zip(gains_0, gains_1))
    first_re = gain_re[:, 0:1]
    first_im = gain_im[:, 0:1]
    divisor = jnp.maximum(jnp.sqrt(first_re * first_re + first_im * first_im), 1.0)
    unit_re = first_re / divisor
    unit_im = -first_im / divisor
    mine[0] = gain_re * unit_re - gain_im * unit_im
    mine[1] = gain_re * unit_im + gain_im * unit_re

    pl.semaphore_wait(barrier, 2)
    copies = [
        pltpu.make_async_remote_copy(
            src_ref=mine,
            dst_ref=halo.at[slot],
            send_sem=send_sem.at[slot],
            recv_sem=recv_sem.at[slot],
            device_id=other,
            device_id_type=MESH,
        )
        for slot, other in ((0, right), (1, left))
    ]
    for copy in copies:
        copy.start()
    width_copy.wait()
    row = lax.broadcasted_iota(jnp.int32, (MATS, N), 0)
    within = lax.rem(row, LT)
    interval = me * LT + within
    half_width = jnp.where(row < LT, width[0], width[1])
    for copy in copies:
        copy.wait()

    def moved(x, offset):
        return x if offset % MATS == 0 else jnp.concatenate([x[offset % MATS :], x[: offset % MATS]], axis=0)

    sums = []
    for part in range(2):
        here = mine[part]
        before = halo[0, part]
        after = halo[1, part]
        total = jnp.zeros((MATS, N), F32)
        count = jnp.zeros((MATS, N), F32)
        for offset in range(-HW, HW + 1):
            value = moved(here, offset)
            if offset > 0:
                value = jnp.where(within + offset < LT, value, moved(after, offset - LT))
            if offset < 0:
                value = jnp.where(within + offset >= 0, value, moved(before, offset + LT))
            inside = (half_width >= abs(offset)) & (interval + offset >= 0) & (interval + offset < ALL_T)
            total = total + jnp.where(inside, value, 0.0)
            count = count + jnp.where(inside, 1.0, 0.0)
        sums.append(total / count)
    smooth_re, smooth_im = sums
    size = jnp.maximum(smooth_re * smooth_re + smooth_im * smooth_im, 1.0)
    inv_ref[0] = smooth_re / size
    inv_ref[1] = -smooth_im / size


def inverse_gains(widths, vis, mod):
    hbm = pl.BlockSpec(memory_space=pltpu.HBM)
    vmem = pl.BlockSpec(memory_space=pltpu.VMEM)
    return pl.pallas_call(
        gains_kernel,
        in_specs=[hbm, hbm, hbm],
        out_specs=[vmem, vmem],
        out_shape=[
            jax.ShapeDtypeStruct((2, MATS, N), F32),
            jax.ShapeDtypeStruct((MATS, 2, N, N), BF16),
        ],
        scratch_shapes=[
            pltpu.VMEM((MATS, 2, N, N), BF16),
            pltpu.VMEM((LT, 2, N, N), BF16),
            pltpu.VMEM((LT, 2, N, N), BF16),
            pltpu.VMEM((LT, N, N), F32),
            pltpu.VMEM((LT, N, N), F32),
            pltpu.VMEM((2, MATS, N), F32),
            pltpu.VMEM((2, 2, MATS, N), F32),
            pltpu.SMEM((LC,), jnp.int32),
            pltpu.SemaphoreType.DMA((2, MATS)),
            pltpu.SemaphoreType.DMA,
            pltpu.SemaphoreType.DMA((2,)),
            pltpu.SemaphoreType.DMA((2,)),
        ],
        compiler_params=pltpu.CompilerParams(
            collective_id=0, has_side_effects=True, vmem_limit_bytes=34 * MIB
        ),
        name="gains",
    )(*(pltpu.with_memory_space_constraint(x, pltpu.HBM) for x in (widths, vis, mod)))


def sums_kernel(weight_hbm, bank_hbm, inv_ref, vis_ref, out_ref, weight, bank, row_a, row_b, col_a, col_b, sem):
    copies = [
        pltpu.make_async_copy(weight_hbm, weight, sem.at[0]),
        pltpu.make_async_copy(bank_hbm, bank, sem.at[1]),
    ]
    for copy in copies:
        copy.start()
    row = lax.broadcasted_iota(jnp.int32, (16, N), 0)
    groups = N // BLK
    strip = 32

    def stacked(rows):
        out = jnp.zeros((16, N), F32)
        for k, one in enumerate(rows):
            out = jnp.where(row == k, one, out)
        return out

    def factors(m, by_row, by_col):
        re_high, re_low = split(inv_ref[0, pl.ds(m, 1), :])
        im_high, im_low = split(inv_ref[1, pl.ds(m, 1), :])
        by_row[...] = jnp.transpose(stacked([re_high, re_low, re_high, im_high, im_low, im_high])).astype(BF16)
        col_re = stacked([re_high, re_high, re_low, im_high, im_high, im_low]).astype(BF16)
        col_im = stacked([-im_high, -im_high, -im_low, re_high, re_high, re_low]).astype(BF16)
        for j in range(groups):
            cols = slice(j * BLK, (j + 1) * BLK)
            by_col[j, :, 0:BLK] = col_re[:, cols]
            by_col[j, :, BLK : 2 * BLK] = col_im[:, cols]

    def add(m, c, by_row, by_col):
        for j in range(groups):
            cols = slice(j * BLK, (j + 1) * BLK)
            for i in range(groups):
                place = bank[m, i * groups + j] * NWEIGHT + weight[c, i * groups + j]
                scale = jnp.dot(by_row[i * BLK : (i + 1) * BLK, :], by_col[j], preferred_element_type=F32)
                ones = []
                for s in range(0, BLK, strip):
                    rows = slice(i * BLK + s, i * BLK + s + strip)
                    to = slice(s, s + strip)
                    vis_re = vis_ref[m, 0, rows, cols].astype(F32)
                    vis_im = vis_ref[m, 1, rows, cols].astype(F32)
                    one_re = scale[to, 0:BLK]
                    one_im = scale[to, BLK : 2 * BLK]
                    ones.append((to, one_re * vis_re - one_im * vis_im, one_re * vis_im + one_im * vis_re))
                for to, one_re, one_im in ones:
                    out_ref[place, to, 0:BLK] += one_re
                    out_ref[place, to, BLK : 2 * BLK] += one_im

    def clear(k, carry):
        out_ref[k] = jnp.zeros((BLK, 2 * BLK), F32)
        return carry

    factors(0, row_a, col_a)
    lax.fori_loop(0, BANKS * NWEIGHT, clear, 0)
    for copy in copies:
        copy.wait()

    def two(q, carry):
        c = lax.div(q, LT // 2)
        factors(2 * q + 1, row_b, col_b)
        add(2 * q, c, row_a, col_a)
        factors(jnp.minimum(2 * q + 2, MATS - 1), row_a, col_a)
        add(2 * q + 1, c, row_b, col_b)
        return carry

    lax.fori_loop(0, MATS // 2, two, 0)


def calibrated_sums(weight_index, target_bank, inverse, vis):
    hbm = pl.BlockSpec(memory_space=pltpu.HBM)
    vmem = pl.BlockSpec(memory_space=pltpu.VMEM)
    return pl.pallas_call(
        sums_kernel,
        in_specs=[hbm, hbm, vmem, vmem],
        out_specs=vmem,
        out_shape=jax.ShapeDtypeStruct((BANKS * NWEIGHT, BLK, 2 * BLK), F32),
        scratch_shapes=[
            pltpu.SMEM((LC, 16), jnp.int32),
            pltpu.SMEM((MATS, 16), jnp.int32),
            pltpu.VMEM((N, 16), BF16),
            pltpu.VMEM((N, 16), BF16),
            pltpu.VMEM((N // BLK, 16, 2 * BLK), BF16),
            pltpu.VMEM((N // BLK, 16, 2 * BLK), BF16),
            pltpu.SemaphoreType.DMA((2,)),
        ],
        compiler_params=pltpu.CompilerParams(vmem_limit_bytes=12 * MIB),
        name="sums",
    )(*(pltpu.with_memory_space_constraint(x, pltpu.HBM) for x in (weight_index, target_bank)), inverse, vis)


STEPS = (2, 1, 3, 0)
A, B, C = slice(0, 3), slice(3, 6), slice(6, 8)


def beams_kernel(left_ref, right_ref, sums_ref, out_ref, *scratch):
    (lefts, rights, formed, terms, pair) = scratch[0:5]
    (parts_a, first_a, own1_a, second_a, own2_a, last_a) = scratch[5:11]
    (parts_b, first_b, own1_b, second_b, own2_b, last_b) = scratch[11:17]
    (parts_c, first_c, own1_c, second_c, own2_c, last_c) = scratch[17:23]
    share = scratch[23]
    sems = scratch[24:]
    (s_pair, s_a1, s_a2, s_a3, s_b1, s_b2, s_b3, s_c1, s_c2, s_c3, s_all) = sems[0:11]
    (r_pair, r_a1, r_a2, r_a3, r_b1, r_b2, r_b3, r_c1, r_c2, r_c3, r_all) = sems[11:22]

    chan = lax.axis_index("chan")
    tm = lax.axis_index("tm")
    z = lax.div(chan, 8)
    y = lax.rem(lax.div(chan, 2), 4)
    x_low = lax.div(tm, 2)
    x = lax.rem(chan, 2) * 2 + x_low
    core = lax.rem(tm, 2)
    place = {"x": x, "y": y, "z": z}

    def device(at, which=core):
        return (
            (at["z"] * 4 + at["y"]) * 2 + lax.div(at["x"], 2),
            lax.rem(at["x"], 2) * 2 + which,
        )

    def at(axis, by):
        return lax.rem(place[axis] + by, 4)

    near = {(axis, by): device({**place, axis: at(axis, by)}) for axis in "xyz" for by in (1, 2, 3)}
    twin = device(place, 1 - core)
    x_pair = lax.div(x, 2) * 2
    x_other = 2 - x_pair
    side = {**place, "x": x_pair + 1 - x_low}
    beside = [device({**side, "y": at("y", by)}) for by in range(4)]
    others = [device({**place, "x": x_other + x_low}), device({**place, "x": x_other + 1 - x_low})]

    barrier = pltpu.get_barrier_semaphore()
    partners = [twin, *beside[1:], *near.values()]
    for other in partners:
        pl.semaphore_signal(barrier, inc=1, device_id=other, device_id_type=MESH)

    for w in range(NWEIGHT):
        lefts[w] = jnp.concatenate([left_ref[w], left_ref[w]], axis=1)
        rights[:, w * BLK : (w + 1) * BLK] = right_ref[w]

    def remote(src, dst, send, recv, to):
        return pltpu.make_async_remote_copy(
            src_ref=src, dst_ref=dst, send_sem=send, recv_sem=recv, device_id=to, device_id_type=MESH
        )

    started = []

    def go(copies):
        for copy in copies:
            copy.start()
        started.extend(copies)

    def pair_copy(n):
        return remote(terms.at[n, 1 - core], pair.at[n], s_pair.at[n], r_pair.at[n], twin)

    def bank(n, step):
        k = at("z", STEPS[step]) * 2 + lax.rem(n, 2)
        for w in range(NWEIGHT):
            high, low = split(sums_ref[k * NWEIGHT + w])
            both = jnp.concatenate([high, low], axis=0).astype(BF16)
            one = jnp.dot(lefts[w], both, preferred_element_type=F32).astype(BF16)
            formed[0, :, w * BLK : (w + 1) * BLK] = one[:, 0:BLK]
            formed[1, :, w * BLK : (w + 1) * BLK] = one[:, BLK : 2 * BLK]
        for part in range(2):
            term = lax.dot_general(
                formed[part], rights[...], (((1,), (1,)), ((), ())), preferred_element_type=F32
            )
            for half in range(2):
                cut = term[:, half * BLK : (half + 1) * BLK].reshape((4, 2, 4, 8, BLK))
                for which in range(2):
                    terms[n, which, part, :, half * 4 : half * 4 + 4] = cut[:, which]

    def compute(step):
        if step == 0:
            bank(0, 0)
            pl.semaphore_wait(barrier, len(partners))
            pair_copy(0).start()

        def one(n, carry):
            bank(n, step)
            pair_copy(n).start()
            return carry

        lax.fori_loop(max(2 * step, 1), 2 * step + 2, one, 0)

    def first_copies(step, axis, parts, first, send, recv):
        return [
            remote(
                parts.at[step, at(axis, by)], first.at[step, n], send.at[step, n], recv.at[step, n], near[axis, by]
            )
            for n, by in enumerate((2, 1, 3))
        ]

    @functools.cache
    def group_a(step):
        return first_copies(step, "x", parts_a, first_a, s_a1, r_a1)

    @functools.cache
    def group_b(step):
        return first_copies(step, "y", parts_b, first_b, s_b1, r_b1)

    @functools.cache
    def c1_copy(step):
        return along_z(step, parts_c, first_c, s_c1, r_c1)

    def pair_sum(step):
        for h in range(2):
            n = 2 * step + h
            pair_copy(n).wait_recv()
            for part in range(2):
                both = terms[n, core, part] + pair[n, part]
                row = 2 * h + part
                parts_a[step, :, row] = both[:, A]
                parts_b[step, row] = both[:, B]
                parts_c[step, :, row] = both[:, C]
        go(group_a(step) + group_b(step))
        if step != 3:
            go([c1_copy(step)])

    def spread(source, axis, slots, send, recv):
        return [
            remote(source.at[at(axis, by)], slots.at[n], send.at[n], recv.at[n], near[axis, by])
            for n, by in enumerate((2, 1, 3))
        ]

    def along_z(step, source, slots, send, recv):
        return remote(source.at[step], slots.at[step], send.at[step], recv.at[step], near["z", STEPS[step]])

    @functools.cache
    def a2_copy(step):
        return along_z(step, own1_a, second_a, s_a2, r_a2)

    def both_chips(source, slots, send, recv):
        copy = lambda n, by, slot, to: remote(source.at[at("y", by)], slots.at[slot], send.at[n], recv.at[n], to)
        made = [copy(n, by, n, near["y", by]) for n, by in enumerate((2, 1, 3))]
        return made + [copy(3 + by, by, 3 + by, beside[by]) for by in (2, 1, 3, 0)]

    @functools.cache
    def a3_copies():
        return both_chips(own2_a, last_a, s_a3, r_a3)

    @functools.cache
    def b2_copy(step):
        return along_z(step, own1_b, second_b, s_b2, r_b2)

    @functools.cache
    def b3_copies():
        pairs = ((x_other, others[1]), (x_other, others[0]), (x_pair, beside[0]))
        return [
            remote(own2_b.at[pl.ds(at_x, 2)], last_b.at[n], s_b3.at[n], r_b3.at[n], to)
            for n, (at_x, to) in enumerate(pairs)
        ]

    @functools.cache
    def c2_copies():
        return spread(own1_c, "x", second_c, s_c2, r_c2)

    @functools.cache
    def c3_copies():
        return both_chips(own2_c, last_c, s_c3, r_c3)

    def arrived(copies):
        for copy in copies:
            copy.wait_recv()

    def finish_first(step):
        arrived(group_a(step))
        total = parts_a[step, x]
        for n in range(3):
            total = total + first_a[step, n]
        own1_a[step] = total
        if step != 3:
            go([a2_copy(step)])
        arrived(group_b(step))
        total = parts_b[step, y]
        for n in range(3):
            total = total + first_b[step, n]
        own1_b[step] = total
        if step != 3:
            go([b2_copy(step)])

    compute(0)
    compute(1)
    pair_sum(0)
    compute(2)
    pair_sum(1)
    compute(3)
    pair_sum(2)
    pair_sum(3)
    finish_first(0)
    finish_first(1)
    finish_first(2)
    arrived([c1_copy(step) for step in range(3)])
    own1_c[...] = parts_c[3] + first_c[0] + first_c[1] + first_c[2]
    go(c2_copies())
    finish_first(3)
    arrived([a2_copy(step) for step in range(3)])
    own2_a[...] = own1_a[3] + second_a[0] + second_a[1] + second_a[2]
    go(a3_copies())
    arrived([b2_copy(step) for step in range(3)])
    own2_b[...] = own1_b[3] + second_b[0] + second_b[1] + second_b[2]
    go(b3_copies())
    arrived(c2_copies())
    own2_c[...] = own1_c[x] + second_c[0] + second_c[1] + second_c[2]
    go(c3_copies())

    def settle(tiles, source, slots):
        share[core, x_low, tiles] = source[y] + slots[0] + slots[1] + slots[2]
        share[core, 1 - x_low, tiles] = slots[3] + slots[4] + slots[5] + slots[6]

    arrived(a3_copies())
    settle(A, own2_a, last_a)
    arrived(b3_copies())
    share[core, :, B] = own2_b[pl.ds(x_pair, 2)] + last_b[0] + last_b[1] + last_b[2]
    arrived(c3_copies())
    settle(C, own2_c, last_c)

    gathers = [remote(share.at[core], share.at[core], s_all, r_all, twin)]
    for copy in gathers:
        copy.start()
    for n in range(BANKS):
        pair_copy(n).wait_send()
    for copy in started:
        copy.wait_send()
    for copy in gathers:
        copy.wait_recv()
    for t in range(TMS):
        for half in range(2):
            for r in range(4):
                rows = slice(t * 32 + r * 8, t * 32 + r * 8 + 8)
                out_ref[rows, half * BLK : (half + 1) * BLK] = share[t % 2, t // 2, half * 4 + r]
    for copy in gathers:
        copy.wait_send()


def beam_banks(left, right, sums):
    tile = (8, BLK)
    vmem = lambda *dims: pltpu.VMEM(dims + tile, F32)
    dma = lambda *dims: pltpu.SemaphoreType.DMA(dims)
    scratch = [
        pltpu.VMEM((NWEIGHT, BEAMS, 2 * BLK), BF16),
        pltpu.VMEM((BEAMS, NWEIGHT * BLK), BF16),
        pltpu.VMEM((2, BEAMS, NWEIGHT * BLK), BF16),
        vmem(BANKS, 2, 2, 4, 8),
        vmem(BANKS, 2, 4, 8),
    ]
    scratch += [vmem(4, 4, 4, 3), vmem(4, 3, 4, 3), vmem(4, 4, 3), vmem(3, 4, 3), vmem(4, 3), vmem(7, 3)]
    scratch += [vmem(4, 4, 4, 3), vmem(4, 3, 4, 3), vmem(4, 4, 3), vmem(3, 4, 3), vmem(4, 3), vmem(3, 2, 3)]
    scratch += [vmem(4, 4, 4, 2), vmem(3, 4, 4, 2), vmem(4, 4, 2), vmem(3, 4, 2), vmem(4, 2), vmem(7, 2)]
    scratch += [vmem(2, 2, 8)]
    sems = [dma(BANKS), dma(4, 3), dma(3), dma(7), dma(4, 3), dma(3), dma(3), dma(3), dma(3), dma(7)]
    sems += [pltpu.SemaphoreType.DMA]
    return pl.pallas_call(
        beams_kernel,
        in_specs=[pl.BlockSpec(memory_space=pltpu.VMEM)] * 3,
        out_specs=pl.BlockSpec(memory_space=pltpu.VMEM),
        out_shape=jax.ShapeDtypeStruct((BLK, BEAMS), F32),
        scratch_shapes=scratch + sems + sems,
        compiler_params=pltpu.CompilerParams(
            collective_id=1, has_side_effects=True, vmem_limit_bytes=24 * MIB
        ),
        name="beams",
    )(left, right, sums)


def local(visibilities, model, beam_left, beam_right, weight_index, target_bank, widths):
    vis = visibilities.reshape((MATS, 2, N, N))
    mod = model.reshape((MATS, 2, N, N))
    inverse, vis = inverse_gains(widths, vis, mod)
    sums = calibrated_sums(weight_index, target_bank.reshape((MATS, 16)), inverse, vis)
    return beam_banks(beam_left, beam_right, sums)


def solution(mesh):
    return jax.shard_map(
        local,
        mesh=mesh,
        in_specs=(
            P("chan", "tm", None, None, None),
            P("chan", "tm", None, None, None),
            P(),
            P(),
            P("chan", None),
            P("chan", "tm", None),
            P("chan"),
        ),
        out_specs=P("chan", None),
        check_vma=False,
    )
```

```python
import functools

import jax
import jax.numpy as jnp
from jax import lax
from jax.experimental import pallas as pl
from jax.experimental.pallas import tpu as pltpu
from jax.sharding import PartitionSpec as P

N = 512
BLK = 128
BEAMS = 256
BANKS = 8
NWEIGHT = 8
ITERS = 6
HW = 2
LC = 2
LT = 4
TMS = 4
ALL_T = 16
MATS = LC * LT
EXACT = 4
FINE = 256
MESH = pl.DeviceIdType.MESH
MIB = 1024 * 1024
F32 = jnp.float32
BF16 = jnp.bfloat16

epsilon = 1e-06


def split(x):
    high = x.astype(BF16).astype(F32)
    return high, x - high


def gains_kernel(
    width_hbm, vis_hbm, mod_hbm, inv_ref, vis_ref,
    mod, cross_0, cross_1, low_0, low_1, power_0, power_1, mine, halo, width, load_sem, width_sem, send_sem, recv_sem,
):
    me = lax.axis_index("tm")
    chan = lax.axis_index("chan")
    right = (chan, lax.rem(me + 1, TMS))
    left = (chan, lax.rem(me + TMS - 1, TMS))
    barrier = pltpu.get_barrier_semaphore()
    for other in (left, right):
        pl.semaphore_signal(barrier, inc=1, device_id=other, device_id_type=MESH)

    def load(m):
        return (
            pltpu.make_async_copy(vis_hbm.at[m], vis_ref.at[m], load_sem.at[0, m]),
            pltpu.make_async_copy(mod_hbm.at[m], mod.at[m], load_sem.at[1, m]),
        )

    for m in range(MATS):
        for copy in load(m):
            copy.start()
    width_copy = pltpu.make_async_copy(width_hbm, width, width_sem)
    width_copy.start()

    row = lax.broadcasted_iota(jnp.int32, (LT, N), 0)
    zeros = jnp.zeros((LT, N), F32)
    strip = 16
    strips = N // strip

    def form(m, slot, top, cross, low, power):
        rows = pl.ds(top, strip)
        fine = top < FINE
        vis_re = vis_ref[m, 0, rows, :].astype(F32)
        vis_im = vis_ref[m, 1, rows, :].astype(F32)
        mod_re = mod[m, 0, rows, :].astype(F32)
        mod_im = mod[m, 1, rows, :].astype(F32)
        cross_re = mod_re * vis_re + mod_im * vis_im
        cross_im = mod_im * vis_re - mod_re * vis_im
        size = mod_re * mod_re + mod_im * mod_im
        for part, one in enumerate((cross_re, cross_im)):
            rounded = one.astype(BF16)
            cross[slot, part, rows, :] = rounded
            if fine:
                low[slot, part, rows, :] = (one - rounded.astype(F32)).astype(BF16)
        power[slot, rows, :] = size
        return [jnp.sum(one.reshape((strip // 8, 8, N)), axis=0) for one in (cross_re, cross_im, size)]

    def spread(totals, sums, slot):
        here = row == slot
        return tuple(
            jnp.where(here, jnp.sum(total, axis=0, keepdims=True), old) for total, old in zip(totals, sums)
        )

    def loaded(m):
        for copy in load(m):
            copy.wait()

    def form_whole(m, sums):
        loaded(m)
        totals = [jnp.zeros((8, N), F32) for _ in range(3)]
        for top in range(0, N, strip):
            totals = [old + new for old, new in zip(totals, form(m, m, top, cross_0, low_0, power_0))]
        return spread(totals, sums, m)

    def sweep(k, gains, cross, low, power, exact, beside=lambda piece: None):
        gain_re, gain_im = gains
        size = gain_re * gain_re + gain_im * gain_im
        by_row = jnp.transpose(jnp.concatenate([size, size], axis=0))
        both = jnp.concatenate([*split(gain_re), *split(gain_im)], axis=0).astype(BF16)
        num_re, num_im, den = zeros, zeros, zeros
        for m in range(LT):
            halves = []
            for part in range(2):
                for half in range(2):
                    columns = slice(half * (N // 2), (half + 1) * (N // 2))
                    one = jnp.dot(both, cross[m, part, :, columns], preferred_element_type=F32)
                    if exact:
                        one = one + jnp.dot(both[:, 0:FINE], low[m, part, :, columns], preferred_element_type=F32)
                    halves.append(one)
                    beside(4 * m + 2 * part + half)
            with_re = jnp.concatenate(halves[0:2], axis=1)
            with_im = jnp.concatenate(halves[2:4], axis=1)
            one_re = (with_re[0:4] + with_re[4:8]) - (with_im[8:12] + with_im[12:16])
            one_im = (with_im[0:4] + with_im[4:8]) + (with_re[8:12] + with_re[12:16])
            total = jnp.zeros((8, N), F32)
            for top in range(0, N, strip):
                rows = slice(top, top + strip)
                total = total + jnp.sum((by_row[rows, m : m + 1] * power[m, rows, :]).reshape((strip // 8, 8, N)), axis=0)
            here = row == m
            num_re = jnp.where(here, one_re, num_re)
            num_im = jnp.where(here, one_im, num_im)
            den = jnp.where(here, jnp.sum(total, axis=0, keepdims=True), den)
        den = den + epsilon
        new_re = num_re / den
        new_im = num_im / den
        odd = lax.rem(k, 2) == 1
        return jnp.where(odd, 0.5 * (new_re + gain_re), new_re), jnp.where(odd, 0.5 * (new_im + gain_im), new_im)

    num_re, num_im, den = lax.fori_loop(0, LT, form_whole, (zeros, zeros, zeros))
    den = den + epsilon
    gains_0 = (num_re / den, num_im / den)
    sums = (zeros, zeros, zeros)
    totals = []
    pieces = (ITERS - 1) * LT * 4

    for k in range(1, ITERS):
        if k <= LT:
            loaded(LT + k - 1)

        def more(piece):
            nonlocal sums, totals
            piece += (k - 1) * LT * 4
            for unit in range(piece * LT * strips // pieces, (piece + 1) * LT * strips // pieces):
                slot, part = divmod(unit, strips)
                new = form(LT + slot, slot, part * strip, cross_1, low_1, power_1)
                totals = new if part == 0 else [old + one for old, one in zip(totals, new)]
                if part == strips - 1:
                    sums = spread(totals, sums, slot)

        gains_0 = sweep(k, gains_0, cross_0, low_0, power_0, k == EXACT, more)

    num_re, num_im, den = sums
    den = den + epsilon
    gains_1 = (num_re / den, num_im / den)
    rounded = lambda k, gains: sweep(k, gains, cross_1, low_1, power_1, False)
    gains_1 = lax.fori_loop(1, EXACT, rounded, gains_1)
    gains_1 = sweep(EXACT, gains_1, cross_1, low_1, power_1, True)
    gains_1 = lax.fori_loop(EXACT + 1, ITERS, rounded, gains_1)
    gain_re, gain_im = (jnp.concatenate(pair, axis=0) for pair in zip(gains_0, gains_1))
    first_re = gain_re[:, 0:1]
    first_im = gain_im[:, 0:1]
    divisor = jnp.maximum(jnp.sqrt(first_re * first_re + first_im * first_im), 1.0)
    unit_re = first_re / divisor
    unit_im = -first_im / divisor
    mine[0] = gain_re * unit_re - gain_im * unit_im
    mine[1] = gain_re * unit_im + gain_im * unit_re

    pl.semaphore_wait(barrier, 2)
    copies = [
        pltpu.make_async_remote_copy(
            src_ref=mine,
            dst_ref=halo.at[slot],
            send_sem=send_sem.at[slot],
            recv_sem=recv_sem.at[slot],
            device_id=other,
            device_id_type=MESH,
        )
        for slot, other in ((0, right), (1, left))
    ]
    for copy in copies:
        copy.start()
    width_copy.wait()
    row = lax.broadcasted_iota(jnp.int32, (MATS, N), 0)
    within = lax.rem(row, LT)
    interval = me * LT + within
    half_width = jnp.where(row < LT, width[0], width[1])
    for copy in copies:
        copy.wait()

    def moved(x, offset):
        return x if offset % MATS == 0 else jnp.concatenate([x[offset % MATS :], x[: offset % MATS]], axis=0)

    sums = []
    for part in range(2):
        here = mine[part]
        before = halo[0, part]
        after = halo[1, part]
        total = jnp.zeros((MATS, N), F32)
        count = jnp.zeros((MATS, N), F32)
        for offset in range(-HW, HW + 1):
            value = moved(here, offset)
            if offset > 0:
                value = jnp.where(within + offset < LT, value, moved(after, offset - LT))
            if offset < 0:
                value = jnp.where(within + offset >= 0, value, moved(before, offset + LT))
            inside = (half_width >= abs(offset)) & (interval + offset >= 0) & (interval + offset < ALL_T)
            total = total + jnp.where(inside, value, 0.0)
            count = count + jnp.where(inside, 1.0, 0.0)
        sums.append(total / count)
    smooth_re, smooth_im = sums
    size = jnp.maximum(smooth_re * smooth_re + smooth_im * smooth_im, 1.0)
    inv_ref[0] = smooth_re / size
    inv_ref[1] = -smooth_im / size


def inverse_gains(widths, vis, mod):
    hbm = pl.BlockSpec(memory_space=pltpu.HBM)
    vmem = pl.BlockSpec(memory_space=pltpu.VMEM)
    return pl.pallas_call(
        gains_kernel,
        in_specs=[hbm, hbm, hbm],
        out_specs=[vmem, vmem],
        out_shape=[
            jax.ShapeDtypeStruct((2, MATS, N), F32),
            jax.ShapeDtypeStruct((MATS, 2, N, N), BF16),
        ],
        scratch_shapes=[
            pltpu.VMEM((MATS, 2, N, N), BF16),
            pltpu.VMEM((LT, 2, N, N), BF16),
            pltpu.VMEM((LT, 2, N, N), BF16),
            pltpu.VMEM((LT, 2, FINE, N), BF16),
            pltpu.VMEM((LT, 2, FINE, N), BF16),
            pltpu.VMEM((LT, N, N), F32),
            pltpu.VMEM((LT, N, N), F32),
            pltpu.VMEM((2, MATS, N), F32),
            pltpu.VMEM((2, 2, MATS, N), F32),
            pltpu.SMEM((LC,), jnp.int32),
            pltpu.SemaphoreType.DMA((2, MATS)),
            pltpu.SemaphoreType.DMA,
            pltpu.SemaphoreType.DMA((2,)),
            pltpu.SemaphoreType.DMA((2,)),
        ],
        compiler_params=pltpu.CompilerParams(
            collective_id=0, has_side_effects=True, vmem_limit_bytes=36 * MIB
        ),
        name="gains",
    )(*(pltpu.with_memory_space_constraint(x, pltpu.HBM) for x in (widths, vis, mod)))


def sums_kernel(weight_hbm, bank_hbm, inv_ref, vis_ref, out_ref, weight, bank, row_a, row_b, col_a, col_b, sem):
    copies = [
        pltpu.make_async_copy(weight_hbm, weight, sem.at[0]),
        pltpu.make_async_copy(bank_hbm, bank, sem.at[1]),
    ]
    for copy in copies:
        copy.start()
    row = lax.broadcasted_iota(jnp.int32, (16, N), 0)
    groups = N // BLK
    strip = 32

    def stacked(rows):
        out = jnp.zeros((16, N), F32)
        for k, one in enumerate(rows):
            out = jnp.where(row == k, one, out)
        return out

    def factors(m, by_row, by_col):
        re_high, re_low = split(inv_ref[0, pl.ds(m, 1), :])
        im_high, im_low = split(inv_ref[1, pl.ds(m, 1), :])
        by_row[...] = jnp.transpose(stacked([re_high, re_low, re_high, im_high, im_low, im_high])).astype(BF16)
        col_re = stacked([re_high, re_high, re_low, im_high, im_high, im_low]).astype(BF16)
        col_im = stacked([-im_high, -im_high, -im_low, re_high, re_high, re_low]).astype(BF16)
        for j in range(groups):
            cols = slice(j * BLK, (j + 1) * BLK)
            by_col[j, :, 0:BLK] = col_re[:, cols]
            by_col[j, :, BLK : 2 * BLK] = col_im[:, cols]

    def add(m, c, by_row, by_col):
        for j in range(groups):
            cols = slice(j * BLK, (j + 1) * BLK)
            for i in range(groups):
                place = bank[m, i * groups + j] * NWEIGHT + weight[c, i * groups + j]
                scale = jnp.dot(by_row[i * BLK : (i + 1) * BLK, :], by_col[j], preferred_element_type=F32)
                ones = []
                for s in range(0, BLK, strip):
                    rows = slice(i * BLK + s, i * BLK + s + strip)
                    to = slice(s, s + strip)
                    vis_re = vis_ref[m, 0, rows, cols].astype(F32)
                    vis_im = vis_ref[m, 1, rows, cols].astype(F32)
                    one_re = scale[to, 0:BLK]
                    one_im = scale[to, BLK : 2 * BLK]
                    ones.append((to, one_re * vis_re - one_im * vis_im, one_re * vis_im + one_im * vis_re))
                for to, one_re, one_im in ones:
                    out_ref[place, to, 0:BLK] += one_re
                    out_ref[place, to, BLK : 2 * BLK] += one_im

    def clear(k, carry):
        out_ref[k] = jnp.zeros((BLK, 2 * BLK), F32)
        return carry

    factors(0, row_a, col_a)
    lax.fori_loop(0, BANKS * NWEIGHT, clear, 0)
    for copy in copies:
        copy.wait()

    def two(q, carry):
        c = lax.div(q, LT // 2)
        factors(2 * q + 1, row_b, col_b)
        add(2 * q, c, row_a, col_a)
        factors(jnp.minimum(2 * q + 2, MATS - 1), row_a, col_a)
        add(2 * q + 1, c, row_b, col_b)
        return carry

    lax.fori_loop(0, MATS // 2, two, 0)


def calibrated_sums(weight_index, target_bank, inverse, vis):
    hbm = pl.BlockSpec(memory_space=pltpu.HBM)
    vmem = pl.BlockSpec(memory_space=pltpu.VMEM)
    return pl.pallas_call(
        sums_kernel,
        in_specs=[hbm, hbm, vmem, vmem],
        out_specs=vmem,
        out_shape=jax.ShapeDtypeStruct((BANKS * NWEIGHT, BLK, 2 * BLK), F32),
        scratch_shapes=[
            pltpu.SMEM((LC, 16), jnp.int32),
            pltpu.SMEM((MATS, 16), jnp.int32),
            pltpu.VMEM((N, 16), BF16),
            pltpu.VMEM((N, 16), BF16),
            pltpu.VMEM((N // BLK, 16, 2 * BLK), BF16),
            pltpu.VMEM((N // BLK, 16, 2 * BLK), BF16),
            pltpu.SemaphoreType.DMA((2,)),
        ],
        compiler_params=pltpu.CompilerParams(vmem_limit_bytes=12 * MIB),
        name="sums",
    )(*(pltpu.with_memory_space_constraint(x, pltpu.HBM) for x in (weight_index, target_bank)), inverse, vis)


STEPS = (2, 1, 3, 0)
A, B, C = slice(0, 3), slice(3, 6), slice(6, 8)


def beams_kernel(left_ref, right_ref, sums_ref, out_ref, *scratch):
    (lefts, rights, formed, terms, pair) = scratch[0:5]
    (parts_a, first_a, own1_a, second_a, own2_a, last_a) = scratch[5:11]
    (parts_b, first_b, own1_b, second_b, own2_b, last_b) = scratch[11:17]
    (parts_c, first_c, own1_c, second_c, own2_c, last_c) = scratch[17:23]
    share = scratch[23]
    sems = scratch[24:]
    (s_pair, s_a1, s_a2, s_a3, s_b1, s_b2, s_b3, s_c1, s_c2, s_c3, s_all) = sems[0:11]
    (r_pair, r_a1, r_a2, r_a3, r_b1, r_b2, r_b3, r_c1, r_c2, r_c3, r_all) = sems[11:22]

    chan = lax.axis_index("chan")
    tm = lax.axis_index("tm")
    z = lax.div(chan, 8)
    y = lax.rem(lax.div(chan, 2), 4)
    x_low = lax.div(tm, 2)
    x = lax.rem(chan, 2) * 2 + x_low
    core = lax.rem(tm, 2)
    place = {"x": x, "y": y, "z": z}

    def device(at, which=core):
        return (
            (at["z"] * 4 + at["y"]) * 2 + lax.div(at["x"], 2),
            lax.rem(at["x"], 2) * 2 + which,
        )

    def at(axis, by):
        return lax.rem(place[axis] + by, 4)

    near = {(axis, by): device({**place, axis: at(axis, by)}) for axis in "xyz" for by in (1, 2, 3)}
    twin = device(place, 1 - core)
    x_pair = lax.div(x, 2) * 2
    x_other = 2 - x_pair
    side = {**place, "x": x_pair + 1 - x_low}
    beside = [device({**side, "y": at("y", by)}) for by in range(4)]
    others = [device({**place, "x": x_other + x_low}), device({**place, "x": x_other + 1 - x_low})]

    barrier = pltpu.get_barrier_semaphore()
    partners = [twin, *beside[1:], *near.values()]
    for other in partners:
        pl.semaphore_signal(barrier, inc=1, device_id=other, device_id_type=MESH)

    for w in range(NWEIGHT):
        lefts[w] = jnp.concatenate([left_ref[w], left_ref[w]], axis=1)
        rights[:, w * BLK : (w + 1) * BLK] = right_ref[w]

    def remote(src, dst, send, recv, to):
        return pltpu.make_async_remote_copy(
            src_ref=src, dst_ref=dst, send_sem=send, recv_sem=recv, device_id=to, device_id_type=MESH
        )

    started = []

    def go(copies):
        for copy in copies:
            copy.start()
        started.extend(copies)

    def pair_copy(n):
        return remote(terms.at[n, 1 - core], pair.at[n], s_pair.at[n], r_pair.at[n], twin)

    def bank(n, step):
        k = at("z", STEPS[step]) * 2 + lax.rem(n, 2)
        for w in range(NWEIGHT):
            high, low = split(sums_ref[k * NWEIGHT + w])
            both = jnp.concatenate([high, low], axis=0).astype(BF16)
            one = jnp.dot(lefts[w], both, preferred_element_type=F32).astype(BF16)
            formed[0, :, w * BLK : (w + 1) * BLK] = one[:, 0:BLK]
            formed[1, :, w * BLK : (w + 1) * BLK] = one[:, BLK : 2 * BLK]
        for part in range(2):
            term = lax.dot_general(
                formed[part], rights[...], (((1,), (1,)), ((), ())), preferred_element_type=F32
            )
            for half in range(2):
                cut = term[:, half * BLK : (half + 1) * BLK].reshape((4, 2, 4, 8, BLK))
                for which in range(2):
                    terms[n, which, part, :, half * 4 : half * 4 + 4] = cut[:, which]

    def compute(step):
        if step == 0:
            bank(0, 0)
            pl.semaphore_wait(barrier, len(partners))
            pair_copy(0).start()

        def one(n, carry):
            bank(n, step)
            pair_copy(n).start()
            return carry

        lax.fori_loop(max(2 * step, 1), 2 * step + 2, one, 0)

    def first_copies(step, axis, parts, first, send, recv):
        return [
            remote(
                parts.at[step, at(axis, by)], first.at[step, n], send.at[step, n], recv.at[step, n], near[axis, by]
            )
            for n, by in enumerate((2, 1, 3))
        ]

    @functools.cache
    def group_a(step):
        return first_copies(step, "x", parts_a, first_a, s_a1, r_a1)

    @functools.cache
    def group_b(step):
        return first_copies(step, "y", parts_b, first_b, s_b1, r_b1)

    @functools.cache
    def c1_copy(step):
        return along_z(step, parts_c, first_c, s_c1, r_c1)

    def pair_sum(step):
        for h in range(2):
            n = 2 * step + h
            pair_copy(n).wait_recv()
            for part in range(2):
                both = terms[n, core, part] + pair[n, part]
                row = 2 * h + part
                parts_a[step, :, row] = both[:, A]
                parts_b[step, row] = both[:, B]
                parts_c[step, :, row] = both[:, C]
        go(group_a(step) + group_b(step))
        if step != 3:
            go([c1_copy(step)])

    def spread(source, axis, slots, send, recv):
        return [
            remote(source.at[at(axis, by)], slots.at[n], send.at[n], recv.at[n], near[axis, by])
            for n, by in enumerate((2, 1, 3))
        ]

    def along_z(step, source, slots, send, recv):
        return remote(source.at[step], slots.at[step], send.at[step], recv.at[step], near["z", STEPS[step]])

    @functools.cache
    def a2_copy(step):
        return along_z(step, own1_a, second_a, s_a2, r_a2)

    def both_chips(source, slots, send, recv):
        copy = lambda n, by, slot, to: remote(source.at[at("y", by)], slots.at[slot], send.at[n], recv.at[n], to)
        made = [copy(n, by, n, near["y", by]) for n, by in enumerate((2, 1, 3))]
        return made + [copy(3 + by, by, 3 + by, beside[by]) for by in (2, 1, 3, 0)]

    @functools.cache
    def a3_copies():
        return both_chips(own2_a, last_a, s_a3, r_a3)

    @functools.cache
    def b2_copy(step):
        return along_z(step, own1_b, second_b, s_b2, r_b2)

    @functools.cache
    def b3_copies():
        pairs = ((x_other, others[1]), (x_other, others[0]), (x_pair, beside[0]))
        return [
            remote(own2_b.at[pl.ds(at_x, 2)], last_b.at[n], s_b3.at[n], r_b3.at[n], to)
            for n, (at_x, to) in enumerate(pairs)
        ]

    @functools.cache
    def c2_copies():
        return spread(own1_c, "x", second_c, s_c2, r_c2)

    @functools.cache
    def c3_copies():
        return both_chips(own2_c, last_c, s_c3, r_c3)

    def arrived(copies):
        for copy in copies:
            copy.wait_recv()

    def finish_first(step):
        arrived(group_a(step))
        total = parts_a[step, x]
        for n in range(3):
            total = total + first_a[step, n]
        own1_a[step] = total
        if step != 3:
            go([a2_copy(step)])
        arrived(group_b(step))
        total = parts_b[step, y]
        for n in range(3):
            total = total + first_b[step, n]
        own1_b[step] = total
        if step != 3:
            go([b2_copy(step)])

    compute(0)
    compute(1)
    pair_sum(0)
    compute(2)
    pair_sum(1)
    compute(3)
    pair_sum(2)
    pair_sum(3)
    finish_first(0)
    finish_first(1)
    finish_first(2)
    arrived([c1_copy(step) for step in range(3)])
    own1_c[...] = parts_c[3] + first_c[0] + first_c[1] + first_c[2]
    go(c2_copies())
    finish_first(3)
    arrived([a2_copy(step) for step in range(3)])
    own2_a[...] = own1_a[3] + second_a[0] + second_a[1] + second_a[2]
    go(a3_copies())
    arrived([b2_copy(step) for step in range(3)])
    own2_b[...] = own1_b[3] + second_b[0] + second_b[1] + second_b[2]
    go(b3_copies())
    arrived(c2_copies())
    own2_c[...] = own1_c[x] + second_c[0] + second_c[1] + second_c[2]
    go(c3_copies())

    def settle(tiles, source, slots):
        share[core, x_low, tiles] = source[y] + slots[0] + slots[1] + slots[2]
        share[core, 1 - x_low, tiles] = slots[3] + slots[4] + slots[5] + slots[6]

    for n in range(BANKS):
        pair_copy(n).wait_send()
    late = [*a3_copies(), *b3_copies(), *c3_copies()]
    for copy in started[: -len(late)]:
        copy.wait_send()
    arrived(a3_copies())
    settle(A, own2_a, last_a)
    arrived(b3_copies())
    share[core, :, B] = own2_b[pl.ds(x_pair, 2)] + last_b[0] + last_b[1] + last_b[2]
    arrived(c3_copies())
    settle(C, own2_c, last_c)

    gathers = [remote(share.at[core], share.at[core], s_all, r_all, twin)]
    for copy in gathers:
        copy.start()
    for copy in late:
        copy.wait_send()
    for copy in gathers:
        copy.wait_recv()
    for t in range(TMS):
        for half in range(2):
            for r in range(4):
                rows = slice(t * 32 + r * 8, t * 32 + r * 8 + 8)
                out_ref[rows, half * BLK : (half + 1) * BLK] = share[t % 2, t // 2, half * 4 + r]
    for copy in gathers:
        copy.wait_send()


def beam_banks(left, right, sums):
    tile = (8, BLK)
    vmem = lambda *dims: pltpu.VMEM(dims + tile, F32)
    dma = lambda *dims: pltpu.SemaphoreType.DMA(dims)
    scratch = [
        pltpu.VMEM((NWEIGHT, BEAMS, 2 * BLK), BF16),
        pltpu.VMEM((BEAMS, NWEIGHT * BLK), BF16),
        pltpu.VMEM((2, BEAMS, NWEIGHT * BLK), BF16),
        vmem(BANKS, 2, 2, 4, 8),
        vmem(BANKS, 2, 4, 8),
    ]
    scratch += [vmem(4, 4, 4, 3), vmem(4, 3, 4, 3), vmem(4, 4, 3), vmem(3, 4, 3), vmem(4, 3), vmem(7, 3)]
    scratch += [vmem(4, 4, 4, 3), vmem(4, 3, 4, 3), vmem(4, 4, 3), vmem(3, 4, 3), vmem(4, 3), vmem(3, 2, 3)]
    scratch += [vmem(4, 4, 4, 2), vmem(3, 4, 4, 2), vmem(4, 4, 2), vmem(3, 4, 2), vmem(4, 2), vmem(7, 2)]
    scratch += [vmem(2, 2, 8)]
    sems = [dma(BANKS), dma(4, 3), dma(3), dma(7), dma(4, 3), dma(3), dma(3), dma(3), dma(3), dma(7)]
    sems += [pltpu.SemaphoreType.DMA]
    return pl.pallas_call(
        beams_kernel,
        in_specs=[pl.BlockSpec(memory_space=pltpu.VMEM)] * 3,
        out_specs=pl.BlockSpec(memory_space=pltpu.VMEM),
        out_shape=jax.ShapeDtypeStruct((BLK, BEAMS), F32),
        scratch_shapes=scratch + sems + sems,
        compiler_params=pltpu.CompilerParams(
            collective_id=1, has_side_effects=True, vmem_limit_bytes=24 * MIB
        ),
        name="beams",
    )(left, right, sums)


def local(visibilities, model, beam_left, beam_right, weight_index, target_bank, widths):
    vis = visibilities.reshape((MATS, 2, N, N))
    mod = model.reshape((MATS, 2, N, N))
    inverse, vis = inverse_gains(widths, vis, mod)
    sums = calibrated_sums(weight_index, target_bank.reshape((MATS, 16)), inverse, vis)
    return beam_banks(beam_left, beam_right, sums)


def solution(mesh):
    return jax.shard_map(
        local,
        mesh=mesh,
        in_specs=(
            P("chan", "tm", None, None, None),
            P("chan", "tm", None, None, None),
            P(),
            P(),
            P("chan", None),
            P("chan", "tm", None),
            P("chan"),
        ),
        out_specs=P("chan", None),
        check_vma=False,
    )
```

```python
import functools

import jax
import jax.numpy as jnp
from jax import lax
from jax.experimental import pallas as pl
from jax.experimental.pallas import tpu as pltpu
from jax.sharding import PartitionSpec as P

N = 512
BLK = 128
BEAMS = 256
BANKS = 8
NWEIGHT = 8
ITERS = 6
HW = 2
LC = 2
LT = 4
TMS = 4
ALL_T = 16
MATS = LC * LT
EXACT = 4
FINE = 256
MESH = pl.DeviceIdType.MESH
MIB = 1024 * 1024
F32 = jnp.float32
BF16 = jnp.bfloat16

epsilon = 1e-06


def split(x):
    high = x.astype(BF16).astype(F32)
    return high, x - high


def gains_kernel(
    width_hbm, vis_hbm, mod_hbm, inv_ref, vis_ref, wide_ref,
    mod, cross_0, cross_1, low_0, low_1, power_0, power_1, mine, halo, width, load_sem, width_sem, send_sem, recv_sem,
):
    me = lax.axis_index("tm")
    chan = lax.axis_index("chan")
    right = (chan, lax.rem(me + 1, TMS))
    left = (chan, lax.rem(me + TMS - 1, TMS))
    barrier = pltpu.get_barrier_semaphore()
    for other in (left, right):
        pl.semaphore_signal(barrier, inc=1, device_id=other, device_id_type=MESH)

    def load(m):
        return (
            pltpu.make_async_copy(vis_hbm.at[m], vis_ref.at[m], load_sem.at[0, m]),
            pltpu.make_async_copy(mod_hbm.at[m], mod.at[m], load_sem.at[1, m]),
        )

    for m in range(MATS):
        for copy in load(m):
            copy.start()
    width_copy = pltpu.make_async_copy(width_hbm, width, width_sem)
    width_copy.start()

    row = lax.broadcasted_iota(jnp.int32, (LT, N), 0)
    zeros = jnp.zeros((LT, N), F32)
    strip = 16
    strips = N // strip

    def form(m, slot, top, cross, low, power, wide=None):
        rows = pl.ds(top, strip)
        fine = top < FINE
        vis_re = vis_ref[m, 0, rows, :].astype(F32)
        vis_im = vis_ref[m, 1, rows, :].astype(F32)
        mod_re = mod[m, 0, rows, :].astype(F32)
        mod_im = mod[m, 1, rows, :].astype(F32)
        if wide is not None:
            wide[slot, 0, rows, :] = vis_re
            wide[slot, 1, rows, :] = vis_im
        cross_re = mod_re * vis_re + mod_im * vis_im
        cross_im = mod_im * vis_re - mod_re * vis_im
        size = mod_re * mod_re + mod_im * mod_im
        for part, one in enumerate((cross_re, cross_im)):
            rounded = one.astype(BF16)
            cross[slot, part, rows, :] = rounded
            if fine:
                low[slot, part, rows, :] = (one - rounded.astype(F32)).astype(BF16)
        power[slot, rows, :] = size
        return [jnp.sum(one.reshape((strip // 8, 8, N)), axis=0) for one in (cross_re, cross_im, size)]

    def spread(totals, sums, slot):
        here = row == slot
        return tuple(
            jnp.where(here, jnp.sum(total, axis=0, keepdims=True), old) for total, old in zip(totals, sums)
        )

    def loaded(m):
        for copy in load(m):
            copy.wait()

    def form_whole(m, sums):
        loaded(m)
        totals = [jnp.zeros((8, N), F32) for _ in range(3)]
        for top in range(0, N, strip):
            totals = [old + new for old, new in zip(totals, form(m, m, top, cross_0, low_0, power_0, wide_ref))]
        return spread(totals, sums, m)

    def sweep(k, gains, cross, low, power, exact, beside=lambda piece: None):
        gain_re, gain_im = gains
        size = gain_re * gain_re + gain_im * gain_im
        by_row = jnp.transpose(jnp.concatenate([size, size], axis=0))
        both = jnp.concatenate([*split(gain_re), *split(gain_im)], axis=0).astype(BF16)
        num_re, num_im, den = zeros, zeros, zeros
        for m in range(LT):
            halves = []
            for part in range(2):
                for half in range(2):
                    columns = slice(half * (N // 2), (half + 1) * (N // 2))
                    one = jnp.dot(both, cross[m, part, :, columns], preferred_element_type=F32)
                    if exact:
                        one = one + jnp.dot(both[:, 0:FINE], low[m, part, :, columns], preferred_element_type=F32)
                    halves.append(one)
                    beside(4 * m + 2 * part + half)
            with_re = jnp.concatenate(halves[0:2], axis=1)
            with_im = jnp.concatenate(halves[2:4], axis=1)
            one_re = (with_re[0:4] + with_re[4:8]) - (with_im[8:12] + with_im[12:16])
            one_im = (with_im[0:4] + with_im[4:8]) + (with_re[8:12] + with_re[12:16])
            total = jnp.zeros((8, N), F32)
            for top in range(0, N, strip):
                rows = slice(top, top + strip)
                total = total + jnp.sum((by_row[rows, m : m + 1] * power[m, rows, :]).reshape((strip // 8, 8, N)), axis=0)
            here = row == m
            num_re = jnp.where(here, one_re, num_re)
            num_im = jnp.where(here, one_im, num_im)
            den = jnp.where(here, jnp.sum(total, axis=0, keepdims=True), den)
        den = den + epsilon
        new_re = num_re / den
        new_im = num_im / den
        odd = lax.rem(k, 2) == 1
        return jnp.where(odd, 0.5 * (new_re + gain_re), new_re), jnp.where(odd, 0.5 * (new_im + gain_im), new_im)

    num_re, num_im, den = lax.fori_loop(0, LT, form_whole, (zeros, zeros, zeros))
    den = den + epsilon
    gains_0 = (num_re / den, num_im / den)
    sums = (zeros, zeros, zeros)
    totals = []
    pieces = (ITERS - 1) * LT * 4

    for k in range(1, ITERS):
        if k <= LT:
            loaded(LT + k - 1)

        def more(piece):
            nonlocal sums, totals
            piece += (k - 1) * LT * 4
            for unit in range(piece * LT * strips // pieces, (piece + 1) * LT * strips // pieces):
                slot, part = divmod(unit, strips)
                new = form(LT + slot, slot, part * strip, cross_1, low_1, power_1)
                totals = new if part == 0 else [old + one for old, one in zip(totals, new)]
                if part == strips - 1:
                    sums = spread(totals, sums, slot)

        gains_0 = sweep(k, gains_0, cross_0, low_0, power_0, k == EXACT, more)

    num_re, num_im, den = sums
    den = den + epsilon
    gains_1 = (num_re / den, num_im / den)
    rounded = lambda k, gains: sweep(k, gains, cross_1, low_1, power_1, False)
    gains_1 = lax.fori_loop(1, EXACT, rounded, gains_1)
    gains_1 = sweep(EXACT, gains_1, cross_1, low_1, power_1, True)
    gains_1 = lax.fori_loop(EXACT + 1, ITERS, rounded, gains_1)
    gain_re, gain_im = (jnp.concatenate(pair, axis=0) for pair in zip(gains_0, gains_1))
    first_re = gain_re[:, 0:1]
    first_im = gain_im[:, 0:1]
    divisor = jnp.maximum(jnp.sqrt(first_re * first_re + first_im * first_im), 1.0)
    unit_re = first_re / divisor
    unit_im = -first_im / divisor
    mine[0] = gain_re * unit_re - gain_im * unit_im
    mine[1] = gain_re * unit_im + gain_im * unit_re

    pl.semaphore_wait(barrier, 2)
    copies = [
        pltpu.make_async_remote_copy(
            src_ref=mine,
            dst_ref=halo.at[slot],
            send_sem=send_sem.at[slot],
            recv_sem=recv_sem.at[slot],
            device_id=other,
            device_id_type=MESH,
        )
        for slot, other in ((0, right), (1, left))
    ]
    for copy in copies:
        copy.start()
    width_copy.wait()
    row = lax.broadcasted_iota(jnp.int32, (MATS, N), 0)
    within = lax.rem(row, LT)
    interval = me * LT + within
    half_width = jnp.where(row < LT, width[0], width[1])
    for copy in copies:
        copy.wait()

    def moved(x, offset):
        return x if offset % MATS == 0 else jnp.concatenate([x[offset % MATS :], x[: offset % MATS]], axis=0)

    sums = []
    for part in range(2):
        here = mine[part]
        before = halo[0, part]
        after = halo[1, part]
        total = jnp.zeros((MATS, N), F32)
        count = jnp.zeros((MATS, N), F32)
        for offset in range(-HW, HW + 1):
            value = moved(here, offset)
            if offset > 0:
                value = jnp.where(within + offset < LT, value, moved(after, offset - LT))
            if offset < 0:
                value = jnp.where(within + offset >= 0, value, moved(before, offset + LT))
            inside = (half_width >= abs(offset)) & (interval + offset >= 0) & (interval + offset < ALL_T)
            total = total + jnp.where(inside, value, 0.0)
            count = count + jnp.where(inside, 1.0, 0.0)
        sums.append(total / count)
    smooth_re, smooth_im = sums
    size = jnp.maximum(smooth_re * smooth_re + smooth_im * smooth_im, 1.0)
    inv_ref[0] = smooth_re / size
    inv_ref[1] = -smooth_im / size


def inverse_gains(widths, vis, mod):
    hbm = pl.BlockSpec(memory_space=pltpu.HBM)
    vmem = pl.BlockSpec(memory_space=pltpu.VMEM)
    return pl.pallas_call(
        gains_kernel,
        in_specs=[hbm, hbm, hbm],
        out_specs=[vmem, vmem, vmem],
        out_shape=[
            jax.ShapeDtypeStruct((2, MATS, N), F32),
            jax.ShapeDtypeStruct((MATS, 2, N, N), BF16),
            jax.ShapeDtypeStruct((LT, 2, N, N), F32),
        ],
        scratch_shapes=[
            pltpu.VMEM((MATS, 2, N, N), BF16),
            pltpu.VMEM((LT, 2, N, N), BF16),
            pltpu.VMEM((LT, 2, N, N), BF16),
            pltpu.VMEM((LT, 2, FINE, N), BF16),
            pltpu.VMEM((LT, 2, FINE, N), BF16),
            pltpu.VMEM((LT, N, N), F32),
            pltpu.VMEM((LT, N, N), F32),
            pltpu.VMEM((2, MATS, N), F32),
            pltpu.VMEM((2, 2, MATS, N), F32),
            pltpu.SMEM((LC,), jnp.int32),
            pltpu.SemaphoreType.DMA((2, MATS)),
            pltpu.SemaphoreType.DMA,
            pltpu.SemaphoreType.DMA((2,)),
            pltpu.SemaphoreType.DMA((2,)),
        ],
        compiler_params=pltpu.CompilerParams(
            collective_id=0, has_side_effects=True, vmem_limit_bytes=36 * MIB
        ),
        name="gains",
    )(*(pltpu.with_memory_space_constraint(x, pltpu.HBM) for x in (widths, vis, mod)))


def sums_kernel(weight_hbm, bank_hbm, inv_ref, vis_ref, wide_ref, out_ref, weight, bank, row_a, row_b, col_a, col_b, sem):
    copies = [
        pltpu.make_async_copy(weight_hbm, weight, sem.at[0]),
        pltpu.make_async_copy(bank_hbm, bank, sem.at[1]),
    ]
    for copy in copies:
        copy.start()
    row = lax.broadcasted_iota(jnp.int32, (16, N), 0)
    groups = N // BLK
    strip = 32

    def stacked(rows):
        out = jnp.zeros((16, N), F32)
        for k, one in enumerate(rows):
            out = jnp.where(row == k, one, out)
        return out

    def factors(m, by_row, by_col):
        re_high, re_low = split(inv_ref[0, pl.ds(m, 1), :])
        im_high, im_low = split(inv_ref[1, pl.ds(m, 1), :])
        by_row[...] = jnp.transpose(stacked([re_high, re_low, re_high, im_high, im_low, im_high])).astype(BF16)
        col_re = stacked([re_high, re_high, re_low, im_high, im_high, im_low]).astype(BF16)
        col_im = stacked([-im_high, -im_high, -im_low, re_high, re_high, re_low]).astype(BF16)
        for j in range(groups):
            cols = slice(j * BLK, (j + 1) * BLK)
            by_col[j, :, 0:BLK] = col_re[:, cols]
            by_col[j, :, BLK : 2 * BLK] = col_im[:, cols]

    def add(m, c, by_row, by_col, vis):
        for j in range(groups):
            cols = slice(j * BLK, (j + 1) * BLK)
            for i in range(groups):
                place = bank[m, i * groups + j] * NWEIGHT + weight[c, i * groups + j]
                scale = jnp.dot(by_row[i * BLK : (i + 1) * BLK, :], by_col[j], preferred_element_type=F32)
                ones = []
                for s in range(0, BLK, strip):
                    rows = slice(i * BLK + s, i * BLK + s + strip)
                    to = slice(s, s + strip)
                    vis_re = vis[m, 0, rows, cols].astype(F32)
                    vis_im = vis[m, 1, rows, cols].astype(F32)
                    one_re = scale[to, 0:BLK]
                    one_im = scale[to, BLK : 2 * BLK]
                    ones.append((to, one_re * vis_re - one_im * vis_im, one_re * vis_im + one_im * vis_re))
                for to, one_re, one_im in ones:
                    out_ref[place, to, 0:BLK] += one_re
                    out_ref[place, to, BLK : 2 * BLK] += one_im

    def clear(k, carry):
        out_ref[k] = jnp.zeros((BLK, 2 * BLK), F32)
        return carry

    factors(0, row_a, col_a)
    lax.fori_loop(0, BANKS * NWEIGHT, clear, 0)
    for copy in copies:
        copy.wait()

    def two(q, c, vis):
        factors(2 * q + 1, row_b, col_b)
        add(2 * q, c, row_a, col_a, vis)
        factors(jnp.minimum(2 * q + 2, MATS - 1), row_a, col_a)
        add(2 * q + 1, c, row_b, col_b, vis)

    for c, vis in enumerate((wide_ref, vis_ref)):

        def one(q, carry):
            two(q, c, vis)
            return carry

        lax.fori_loop(c * LT // 2, (c + 1) * LT // 2, one, 0)


def calibrated_sums(weight_index, target_bank, inverse, vis, wide):
    hbm = pl.BlockSpec(memory_space=pltpu.HBM)
    vmem = pl.BlockSpec(memory_space=pltpu.VMEM)
    return pl.pallas_call(
        sums_kernel,
        in_specs=[hbm, hbm, vmem, vmem, vmem],
        out_specs=vmem,
        out_shape=jax.ShapeDtypeStruct((BANKS * NWEIGHT, BLK, 2 * BLK), F32),
        scratch_shapes=[
            pltpu.SMEM((LC, 16), jnp.int32),
            pltpu.SMEM((MATS, 16), jnp.int32),
            pltpu.VMEM((N, 16), BF16),
            pltpu.VMEM((N, 16), BF16),
            pltpu.VMEM((N // BLK, 16, 2 * BLK), BF16),
            pltpu.VMEM((N // BLK, 16, 2 * BLK), BF16),
            pltpu.SemaphoreType.DMA((2,)),
        ],
        compiler_params=pltpu.CompilerParams(vmem_limit_bytes=12 * MIB),
        name="sums",
    )(*(pltpu.with_memory_space_constraint(x, pltpu.HBM) for x in (weight_index, target_bank)), inverse, vis, wide)


STEPS = (2, 1, 3, 0)
A, B, C = slice(0, 3), slice(3, 6), slice(6, 8)


def beams_kernel(left_ref, right_ref, sums_ref, out_ref, *scratch):
    (lefts, rights, formed, terms, pair) = scratch[0:5]
    (parts_a, first_a, own1_a, second_a, own2_a, last_a) = scratch[5:11]
    (parts_b, first_b, own1_b, second_b, own2_b, last_b) = scratch[11:17]
    (parts_c, first_c, own1_c, second_c, own2_c, last_c) = scratch[17:23]
    share = scratch[23]
    sems = scratch[24:]
    (s_pair, s_a1, s_a2, s_a3, s_b1, s_b2, s_b3, s_c1, s_c2, s_c3, s_all) = sems[0:11]
    (r_pair, r_a1, r_a2, r_a3, r_b1, r_b2, r_b3, r_c1, r_c2, r_c3, r_all) = sems[11:22]

    chan = lax.axis_index("chan")
    tm = lax.axis_index("tm")
    z = lax.div(chan, 8)
    y = lax.rem(lax.div(chan, 2), 4)
    x_low = lax.div(tm, 2)
    x = lax.rem(chan, 2) * 2 + x_low
    core = lax.rem(tm, 2)
    place = {"x": x, "y": y, "z": z}

    def device(at, which=core):
        return (
            (at["z"] * 4 + at["y"]) * 2 + lax.div(at["x"], 2),
            lax.rem(at["x"], 2) * 2 + which,
        )

    def at(axis, by):
        return lax.rem(place[axis] + by, 4)

    near = {(axis, by): device({**place, axis: at(axis, by)}) for axis in "xyz" for by in (1, 2, 3)}
    twin = device(place, 1 - core)
    x_pair = lax.div(x, 2) * 2
    x_other = 2 - x_pair
    side = {**place, "x": x_pair + 1 - x_low}
    beside = [device({**side, "y": at("y", by)}) for by in range(4)]
    others = [device({**place, "x": x_other + x_low}), device({**place, "x": x_other + 1 - x_low})]

    barrier = pltpu.get_barrier_semaphore()
    partners = [twin, *beside[1:], *near.values()]
    for other in partners:
        pl.semaphore_signal(barrier, inc=1, device_id=other, device_id_type=MESH)

    for w in range(NWEIGHT):
        lefts[w] = jnp.concatenate([left_ref[w], left_ref[w]], axis=1)
        rights[:, w * BLK : (w + 1) * BLK] = right_ref[w]

    def remote(src, dst, send, recv, to):
        return pltpu.make_async_remote_copy(
            src_ref=src, dst_ref=dst, send_sem=send, recv_sem=recv, device_id=to, device_id_type=MESH
        )

    started = []

    def go(copies):
        for copy in copies:
            copy.start()
        started.extend(copies)

    def pair_copy(n):
        return remote(terms.at[n, 1 - core], pair.at[n], s_pair.at[n], r_pair.at[n], twin)

    def bank(n, step):
        k = at("z", STEPS[step]) * 2 + lax.rem(n, 2)
        for w in range(NWEIGHT):
            high, low = split(sums_ref[k * NWEIGHT + w])
            both = jnp.concatenate([high, low], axis=0).astype(BF16)
            one = jnp.dot(lefts[w], both, preferred_element_type=F32).astype(BF16)
            formed[0, :, w * BLK : (w + 1) * BLK] = one[:, 0:BLK]
            formed[1, :, w * BLK : (w + 1) * BLK] = one[:, BLK : 2 * BLK]
        for part in range(2):
            term = lax.dot_general(
                formed[part], rights[...], (((1,), (1,)), ((), ())), preferred_element_type=F32
            )
            for half in range(2):
                cut = term[:, half * BLK : (half + 1) * BLK].reshape((4, 2, 4, 8, BLK))
                for which in range(2):
                    terms[n, which, part, :, half * 4 : half * 4 + 4] = cut[:, which]

    def compute(step):
        if step == 0:
            bank(0, 0)
            pl.semaphore_wait(barrier, len(partners))
            pair_copy(0).start()

        def one(n, carry):
            bank(n, step)
            pair_copy(n).start()
            return carry

        lax.fori_loop(max(2 * step, 1), 2 * step + 2, one, 0)

    def first_copies(step, axis, parts, first, send, recv):
        return [
            remote(
                parts.at[step, at(axis, by)], first.at[step, n], send.at[step, n], recv.at[step, n], near[axis, by]
            )
            for n, by in enumerate((2, 1, 3))
        ]

    @functools.cache
    def group_a(step):
        return first_copies(step, "x", parts_a, first_a, s_a1, r_a1)

    @functools.cache
    def group_b(step):
        return first_copies(step, "y", parts_b, first_b, s_b1, r_b1)

    @functools.cache
    def c1_copy(step):
        return along_z(step, parts_c, first_c, s_c1, r_c1)

    def pair_sum(step):
        for h in range(2):
            n = 2 * step + h
            pair_copy(n).wait_recv()
            for part in range(2):
                both = terms[n, core, part] + pair[n, part]
                row = 2 * h + part
                parts_a[step, :, row] = both[:, A]
                parts_b[step, row] = both[:, B]
                parts_c[step, :, row] = both[:, C]
        go(group_a(step) + group_b(step))
        if step != 3:
            go([c1_copy(step)])

    def spread(source, axis, slots, send, recv):
        return [
            remote(source.at[at(axis, by)], slots.at[n], send.at[n], recv.at[n], near[axis, by])
            for n, by in enumerate((2, 1, 3))
        ]

    def along_z(step, source, slots, send, recv):
        return remote(source.at[step], slots.at[step], send.at[step], recv.at[step], near["z", STEPS[step]])

    @functools.cache
    def a2_copy(step):
        return along_z(step, own1_a, second_a, s_a2, r_a2)

    def both_chips(source, slots, send, recv):
        copy = lambda n, by, slot, to: remote(source.at[at("y", by)], slots.at[slot], send.at[n], recv.at[n], to)
        made = [copy(n, by, n, near["y", by]) for n, by in enumerate((2, 1, 3))]
        return made + [copy(3 + by, by, 3 + by, beside[by]) for by in (2, 1, 3, 0)]

    @functools.cache
    def a3_copies():
        return both_chips(own2_a, last_a, s_a3, r_a3)

    @functools.cache
    def b2_copy(step):
        return along_z(step, own1_b, second_b, s_b2, r_b2)

    @functools.cache
    def b3_copies():
        pairs = ((x_other, others[1]), (x_other, others[0]), (x_pair, beside[0]))
        return [
            remote(own2_b.at[pl.ds(at_x, 2)], last_b.at[n], s_b3.at[n], r_b3.at[n], to)
            for n, (at_x, to) in enumerate(pairs)
        ]

    @functools.cache
    def c2_copies():
        return spread(own1_c, "x", second_c, s_c2, r_c2)

    @functools.cache
    def c3_copies():
        return both_chips(own2_c, last_c, s_c3, r_c3)

    def arrived(copies):
        for copy in copies:
            copy.wait_recv()

    def finish_first(step):
        arrived(group_a(step))
        total = parts_a[step, x]
        for n in range(3):
            total = total + first_a[step, n]
        own1_a[step] = total
        if step != 3:
            go([a2_copy(step)])
        arrived(group_b(step))
        total = parts_b[step, y]
        for n in range(3):
            total = total + first_b[step, n]
        own1_b[step] = total
        if step != 3:
            go([b2_copy(step)])

    compute(0)
    compute(1)
    pair_sum(0)
    compute(2)
    pair_sum(1)
    compute(3)
    pair_sum(2)
    pair_sum(3)
    finish_first(0)
    finish_first(1)
    finish_first(2)
    arrived([c1_copy(step) for step in range(3)])
    own1_c[...] = parts_c[3] + first_c[0] + first_c[1] + first_c[2]
    go(c2_copies())
    finish_first(3)
    arrived([a2_copy(step) for step in range(3)])
    own2_a[...] = own1_a[3] + second_a[0] + second_a[1] + second_a[2]
    go(a3_copies())
    arrived([b2_copy(step) for step in range(3)])
    own2_b[...] = own1_b[3] + second_b[0] + second_b[1] + second_b[2]
    go(b3_copies())
    arrived(c2_copies())
    own2_c[...] = own1_c[x] + second_c[0] + second_c[1] + second_c[2]
    go(c3_copies())

    def settle(tiles, source, slots):
        share[core, x_low, tiles] = source[y] + slots[0] + slots[1] + slots[2]
        share[core, 1 - x_low, tiles] = slots[3] + slots[4] + slots[5] + slots[6]

    for n in range(BANKS):
        pair_copy(n).wait_send()
    late = [*a3_copies(), *b3_copies(), *c3_copies()]
    for copy in started[: -len(late)]:
        copy.wait_send()
    arrived(a3_copies())
    settle(A, own2_a, last_a)
    arrived(b3_copies())
    share[core, :, B] = own2_b[pl.ds(x_pair, 2)] + last_b[0] + last_b[1] + last_b[2]
    arrived(c3_copies())
    settle(C, own2_c, last_c)

    gathers = [remote(share.at[core], share.at[core], s_all, r_all, twin)]
    for copy in gathers:
        copy.start()
    for copy in late:
        copy.wait_send()
    for copy in gathers:
        copy.wait_recv()
    for t in range(TMS):
        for half in range(2):
            for r in range(4):
                rows = slice(t * 32 + r * 8, t * 32 + r * 8 + 8)
                out_ref[rows, half * BLK : (half + 1) * BLK] = share[t % 2, t // 2, half * 4 + r]
    for copy in gathers:
        copy.wait_send()


def beam_banks(left, right, sums):
    tile = (8, BLK)
    vmem = lambda *dims: pltpu.VMEM(dims + tile, F32)
    dma = lambda *dims: pltpu.SemaphoreType.DMA(dims)
    scratch = [
        pltpu.VMEM((NWEIGHT, BEAMS, 2 * BLK), BF16),
        pltpu.VMEM((BEAMS, NWEIGHT * BLK), BF16),
        pltpu.VMEM((2, BEAMS, NWEIGHT * BLK), BF16),
        vmem(BANKS, 2, 2, 4, 8),
        vmem(BANKS, 2, 4, 8),
    ]
    scratch += [vmem(4, 4, 4, 3), vmem(4, 3, 4, 3), vmem(4, 4, 3), vmem(3, 4, 3), vmem(4, 3), vmem(7, 3)]
    scratch += [vmem(4, 4, 4, 3), vmem(4, 3, 4, 3), vmem(4, 4, 3), vmem(3, 4, 3), vmem(4, 3), vmem(3, 2, 3)]
    scratch += [vmem(4, 4, 4, 2), vmem(3, 4, 4, 2), vmem(4, 4, 2), vmem(3, 4, 2), vmem(4, 2), vmem(7, 2)]
    scratch += [vmem(2, 2, 8)]
    sems = [dma(BANKS), dma(4, 3), dma(3), dma(7), dma(4, 3), dma(3), dma(3), dma(3), dma(3), dma(7)]
    sems += [pltpu.SemaphoreType.DMA]
    return pl.pallas_call(
        beams_kernel,
        in_specs=[pl.BlockSpec(memory_space=pltpu.VMEM)] * 3,
        out_specs=pl.BlockSpec(memory_space=pltpu.VMEM),
        out_shape=jax.ShapeDtypeStruct((BLK, BEAMS), F32),
        scratch_shapes=scratch + sems + sems,
        compiler_params=pltpu.CompilerParams(
            collective_id=1, has_side_effects=True, vmem_limit_bytes=24 * MIB
        ),
        name="beams",
    )(left, right, sums)


def local(visibilities, model, beam_left, beam_right, weight_index, target_bank, widths):
    vis = visibilities.reshape((MATS, 2, N, N))
    mod = model.reshape((MATS, 2, N, N))
    inverse, vis, wide = inverse_gains(widths, vis, mod)
    sums = calibrated_sums(weight_index, target_bank.reshape((MATS, 16)), inverse, vis, wide)
    return beam_banks(beam_left, beam_right, sums)


def solution(mesh):
    return jax.shard_map(
        local,
        mesh=mesh,
        in_specs=(
            P("chan", "tm", None, None, None),
            P("chan", "tm", None, None, None),
            P(),
            P(),
            P("chan", None),
            P("chan", "tm", None),
            P("chan"),
        ),
        out_specs=P("chan", None),
        check_vma=False,
    )
```
